1024 devices in a mesh: face: 16 (over x, core), tile: 64 (over z, y).
Axes of the slice: x: 8, y: 8, z: 8, core: 2. Of those that a mesh axis runs over, the one named last changes fastest.
Arguments:
- ocean_forcing: bfloat16 [16, 8192, 4, 128], P('face', 'tile'), may hold values from -5 to 5
- ice_owner: int32 [16, 8192], P('face', 'tile'), may hold values from 0 to 15, as said below
- ice_mask: int32 [16, 8192], P('face', 'tile'), may hold values 0 or 1
- ice_velocity: float32 [2, 16, 512, 2048], P(None, 'face', 'tile'), may hold values from -4 to 4
- ice_mass: float32 [16, 512, 2048], P('face', 'tile'), may hold values from 0.35 to 0.7
- ice_strength: float32 [16, 512, 2048], P('face', 'tile'), may hold values from 1.5 to 3
Outputs:
- velocity_out: float32 [2, 16, 512, 2048], P(None, 'face', 'tile')
- ocean_drag: bfloat16 [16, 8192, 2, 128], P('face', 'tile')
The draws below stay inside these ranges and needn't reach their ends.
Inputs may be any that keep to these rules, and one draw needn't show every extreme that they name: `ice_owner`: within each aligned block of 128 entries of a row (one ocean tile's blocks, aligned), every face index appears exactly 8 times.
All inputs are finite; a program needn't handle non-finite values. No bound on the sum of `ice_mask` on one device may be relied on, other than what follows from the above.
Results may differ from the reference program's by a relative error of at most 0.001.
Values may be sent and summed in bfloat16 or wider, within the bound.
A program may use at most 32 MiB of HBM per device.

```python
import math
import jax
import jax.numpy as jnp
from jax import lax

TY = 8
W = 2048
ITERS = 8
FACES = 16
R = 512
KB = 128
PAIR = 8
KT = 8192


def draw_ice_owner(key, part):
    key = jax.random.fold_in(key, 11)
    rows = FACES * (KT // KB)
    base = jnp.tile((jnp.arange(KB, dtype=jnp.int32) % FACES)[None, :], (rows, 1))
    mixed = jax.random.permutation(key, base, axis=1, independent=True)
    return mixed.reshape(FACES, KT).astype(jnp.int32)


def with_ends(values, stream_key, low, top_value):
    spot = [jax.random.randint(jax.random.fold_in(stream_key, axis), (), 0, length) for axis, length in enumerate(values.shape)]
    longest = values.shape.index(max(values.shape))
    neighbour = spot[:longest] + [(spot[longest] + 1) % values.shape[longest]] + spot[longest + 1:]
    return values.at[tuple(spot)].set(low).at[tuple(neighbour)].set(top_value)


def shard_levels(rng, dims, split, smallest, high):
    gain, own = 1.0, jax.random.fold_in(rng, 6)
    for axis_at, blocks in split:
        steps = jnp.exp(jax.random.uniform(jax.random.fold_in(own, axis_at), (blocks,), jnp.float32, smallest / len(split), high / len(split)))
        gain = gain * jnp.repeat(steps, dims[axis_at] // blocks).reshape([-1 if axis == axis_at else 1 for axis in range(len(dims))])
    return gain


def scatter_about(rng, shape, scale, limit, shards=(), held_as=jnp.bfloat16):
    drawn = scale * jax.random.normal(rng, shape, jnp.float32)
    if shards:
        drawn = drawn * shard_levels(rng, shape, shards, -0.22, 0.18)
    return jnp.clip(drawn, -limit, limit).astype(held_as)


def setup_inputs(seed: int = 0) -> dict:
    key_of = jax.random.split(jax.random.key(seed), 7)
    return {
        "ocean_forcing": scatter_about(key_of[0], (FACES, KT, 4, 128), 0.7, 5.0, ((0, 16), (1, 64))),
        "ice_owner": draw_ice_owner(jax.random.fold_in(key_of[6], 71), 0),
        "ice_mask": with_ends((jax.random.randint(key_of[2], (FACES, KT), 0, 8) < 7).astype(jnp.int32), jax.random.fold_in(key_of[2], 1), 0, 1),
        "ice_velocity": scatter_about(key_of[3], (2, FACES, R, W), 0.5, 4.0, ((1, 16), (2, 64)), jnp.float32),
        "ice_mass": jnp.clip(jnp.exp(math.log(0.7) - 0.6931472 * jax.random.uniform(key_of[4], (FACES, R, W), jnp.float32) ** shard_levels(key_of[4], (FACES, R, W), ((0, 16), (1, 64)), -0.2, 0.2)), 0.35, 0.7),
        "ice_strength": jnp.clip(jnp.exp(math.log(3.0) - 0.6931472 * jax.random.uniform(key_of[5], (FACES, R, W), jnp.float32) ** shard_levels(key_of[5], (FACES, R, W), ((0, 16), (1, 64)), -0.2, 0.2)), 1.5, 3.0),
    }


ECC2 = 4.0
DMIN2 = 0.01
CE = 0.5
DTS = 0.25
CW = 1.0
COR = 0.5

def across_rows(field, signs):
    faces = field.shape[1]
    odd = jnp.arange(faces) % 2 == 1
    lower = jnp.roll(field[:, :, -1, :], 1, axis=1)
    lower_odd = jnp.roll(odd, 1)
    lower = jnp.where(lower_odd[None, :, None], signs[:, None, None] * lower[..., ::-1], lower)
    upper = jnp.roll(field[:, :, 0, :], -1, axis=1)
    upper = jnp.where(odd[None, :, None], signs[:, None, None] * upper[..., ::-1], upper)
    return jnp.concatenate([lower[:, :, None], field, upper[:, :, None]], axis=2)

def slope_x(inner):
    return 0.5 * (jnp.roll(inner, -1, -1) - jnp.roll(inner, 1, -1))

def slope_y(padded):
    return 0.5 * (padded[..., 2:, :] - padded[..., :-2, :])

def stress_update(padded_vel, stress, strength, cover):
    e11 = slope_x(padded_vel[0][..., 1:-1, :])
    e22 = slope_y(padded_vel[1])
    e12 = 0.5 * (slope_y(padded_vel[0]) + slope_x(padded_vel[1][..., 1:-1, :]))
    dd = e11 + e22
    dtn = e11 - e22
    dsh = 2.0 * e12
    delta = jnp.sqrt(dd * dd + (dtn * dtn + dsh * dsh) / ECC2 + DMIN2)
    first = cover * (stress[0] + CE * strength * (dd / delta - 1.0)) / (1.0 + CE)
    second = cover * (stress[1] + CE * strength * dtn / (ECC2 * delta)) / (1.0 + CE)
    shear = cover * (stress[2] + CE * strength * dsh / (2.0 * ECC2 * delta)) / (1.0 + CE)
    return jnp.stack([first, second, shear])

def momentum_update(velocity, padded_stress, mass, forcing, cover):
    s11 = 0.5 * (padded_stress[0] + padded_stress[1])
    s22 = 0.5 * (padded_stress[0] - padded_stress[1])
    s12 = padded_stress[2]
    force_x = slope_x(s11[..., 1:-1, :]) + slope_y(s12)
    force_y = slope_x(s12[..., 1:-1, :]) + slope_y(s22)
    east, north = (velocity[0], velocity[1])
    diff_u = forcing[0] - east
    diff_v = forcing[1] - north
    speed = jnp.sqrt(diff_u * diff_u + diff_v * diff_v)
    damping = 1.0 + DTS * CW * speed / mass
    new_u = cover * (east + DTS / mass * (force_x + forcing[2] + CW * speed * forcing[0] + COR * mass * north)) / damping
    new_v = cover * (north + DTS / mass * (force_y + forcing[3] + CW * speed * forcing[1] - COR * mass * east)) / damping
    return jnp.stack([new_u, new_v])

def drag_of(velocity, forcing, cover):
    diff_u = forcing[0] - velocity[0]
    diff_v = forcing[1] - velocity[1]
    speed = jnp.sqrt(diff_u * diff_u + diff_v * diff_v)
    return jnp.stack([cover * CW * speed * -diff_u, cover * CW * speed * -diff_v]).astype(jnp.bfloat16)

def reference(ocean_forcing, ice_owner, ice_mask, ice_velocity, ice_mass, ice_strength):
    tiles = R // TY
    cols = W // 128
    owner = ice_owner.reshape(FACES, tiles, KB).astype(jnp.int32)
    onehot = (owner[..., None] == jnp.arange(FACES, dtype=jnp.int32)).astype(jnp.int32)
    rank = lax.optimization_barrier(jnp.sum(jnp.cumsum(onehot, axis=2) * onehot, axis=-1)) - 1
    slot = (jnp.arange(FACES, dtype=jnp.int32)[:, None, None] * PAIR + rank).astype(jnp.int32)
    tile_index = jnp.broadcast_to(jnp.arange(tiles, dtype=jnp.int32)[None, :, None], owner.shape)
    blocks = ocean_forcing.reshape(FACES, tiles, KB, 512)
    ice_blocks = jnp.zeros_like(blocks).at[owner, tile_index, slot].set(blocks)
    forcing = ice_blocks.reshape(FACES, tiles, TY, cols, 4, 128).transpose(4, 0, 1, 2, 3, 5)
    forcing = forcing.reshape(4, FACES, R, W).astype(jnp.float32)
    cover = ice_mask.reshape(FACES, R, cols).astype(jnp.float32)
    cover = jnp.repeat(cover, 128, axis=-1)
    vel_signs = jnp.array([-1.0, 1.0], jnp.float32)
    stress_signs = jnp.array([1.0, 1.0, -1.0], jnp.float32)
    velocity = ice_velocity
    stress = jnp.zeros((3, FACES, R, W), jnp.float32)
    for step in range(ITERS):
        stress = stress_update(across_rows(velocity, vel_signs), stress, ice_strength, cover)
        velocity = momentum_update(velocity, across_rows(stress, stress_signs), ice_mass, forcing, cover)
    drag = drag_of(velocity, forcing, cover)
    drag_blocks = drag.reshape(2, FACES, tiles, TY, cols, 128).transpose(1, 2, 3, 4, 0, 5)
    drag_blocks = drag_blocks.reshape(FACES, tiles, KB, 256)
    ocean_drag = drag_blocks[owner, tile_index, slot].reshape(FACES, KT, 2, 128)
    return (velocity, ocean_drag)
```

```python
import functools

import jax
import jax.numpy as jnp
from jax import lax
from jax.experimental import pallas as pl
from jax.experimental.pallas import tpu as pltpu
from jax.sharding import PartitionSpec as P

MESH = pl.DeviceIdType.MESH
F32 = jnp.float32
BF16 = jnp.bfloat16
ROW = 16
OWN = 8 * ROW


def iota(shape, dim):
    return lax.broadcasted_iota(jnp.int32, shape, dim)


def dot(a, b):
    return jnp.dot(a, b, preferred_element_type=F32)


def flip_lanes(x):
    return jnp.take_along_axis(x, 127 - iota(x.shape, 1), axis=1)


def centred_x(x):
    lane = iota(x.shape, 1)
    ahead = pltpu.roll(x, 127, 1)
    behind = pltpu.roll(x, 1, 1)
    ahead = jnp.where(lane == 127, pltpu.roll(ahead, ROW - 1, 0), ahead)
    behind = jnp.where(lane == 0, pltpu.roll(behind, 1, 0), behind)
    return ahead - behind


def rows_of(ref, first, count):
    return [ref[pl.ds(pl.multiple_of((first + n) * ROW, ROW), ROW), :] for n in range(count)]


def put_row(ref, row, value):
    ref[pl.ds(pl.multiple_of(row * ROW, ROW), ROW), :] = value


def stress_rows(first, count, u_ref, v_ref, stress, p_ref):
    us = rows_of(u_ref, first - 1, count + 2)
    vs = rows_of(v_ref, first - 1, count + 2)
    ps = rows_of(p_ref, first, count)
    old = [rows_of(s, first, count) for s in stress]
    third = F32(2.0 / 3.0)
    for n in range(count):
        e11 = centred_x(us[n + 1])
        e22 = vs[n + 2] - vs[n]
        shear = (us[n + 2] - us[n]) + centred_x(vs[n + 1])
        dd = e11 + e22
        dtn = e11 - e22
        inv = lax.rsqrt(dd * dd + 0.25 * (dtn * dtn + shear * shear) + 0.04)
        grip = ps[n] * inv
        put_row(stress[0], first + n, third * old[0][n] + (grip * dd - ps[n]))
        put_row(stress[1], first + n, third * old[1][n] + 0.25 * (grip * dtn))
        put_row(stress[2], first + n, third * old[2][n] + 0.125 * (grip * shear))


def forcing_row(f_ref, row):
    block = f_ref[pl.ds(pl.multiple_of(row * 64, 64), 64), :].astype(F32)
    return [
        jnp.concatenate([block[8 * c : 8 * c + 8], block[32 + 8 * c : 40 + 8 * c]], axis=0)
        for c in range(4)
    ]


def momentum_rows(first, count, cor, u_ref, v_ref, stress, p_ref, m_ref, f_ref):
    s1 = rows_of(stress[0], first - 1, count + 2)
    s2 = rows_of(stress[1], first - 1, count + 2)
    s12 = rows_of(stress[2], first - 1, count + 2)
    us = rows_of(u_ref, first, count)
    vs = rows_of(v_ref, first, count)
    ps = rows_of(p_ref, first, count)
    ms = rows_of(m_ref, first, count)
    for n in range(count):
        uo, vo, tx, ty = forcing_row(f_ref, first + n)
        u, v, m = us[n], vs[n], ms[n]
        fx = 0.25 * centred_x(s1[n + 1] + s2[n + 1]) + 0.5 * (s12[n + 2] - s12[n])
        fy = 0.5 * centred_x(s12[n + 1]) + 0.25 * ((s1[n + 2] - s2[n + 2]) - (s1[n] - s2[n]))
        du = uo - u
        dv = vo - v
        speed = jnp.sqrt(du * du + dv * dv)
        row = first + n
        turn = jnp.where(row < 8, cor[0], jnp.where(row < 16, cor[1], cor[2])) * m
        inv = jnp.where(ps[n] > 0.0, 1.0 / (m + 0.25 * speed), 0.0)
        put_row(u_ref, first + n, (m * u + 0.25 * (fx + tx + speed * uo + turn * v)) * inv)
        put_row(v_ref, first + n, (m * v + 0.25 * (fy + ty + speed * vo - turn * u)) * inv)


def subcycles(cor, u_ref, v_ref, stress, p_ref, m_ref, f_ref):
    def cycle(k, carry):
        first = 1 + 2 * k

        def stress_part(n, c):
            stress_rows(first + 4 * n, 4, u_ref, v_ref, stress, p_ref)
            return c

        def momentum_part(n, c):
            momentum_rows(
                first + 1 + 4 * n, 4, cor, u_ref, v_ref, stress, p_ref, m_ref, f_ref
            )
            return c

        lax.fori_loop(0, 5 - k, stress_part, 0)
        stress_rows(first + 4 * (5 - k), 2, u_ref, v_ref, stress, p_ref)
        lax.fori_loop(0, 5 - k, momentum_part, 0)
        return carry

    lax.fori_loop(0, 4, cycle, 0)


def kernel(
    forcing_hbm, owner_hbm, mask_hbm, vel_hbm, mass_hbm, strength_hbm,
    vel_out, drag_out,
    x_in, owner_in, mask_in, vel_in, mass_in, strength_in,
    spread, send_f, f_all, u1, v1, p_all, m_all, a1, a2, a12,
    u2, v2, b1, b2, b12, send_d, recv_d, unsort, unsorted, drag_buf, vel_buf,
    in_sem, out_sem, f_send, f_recv, h_send, h_recv, g_send, g_recv, k_send, k_recv, d_send, d_recv,
):
    face = lax.axis_index("face")
    tile = lax.axis_index("tile")
    faces = lax.axis_size("face")
    tiles = lax.axis_size("tile")
    ring = face * tiles + tile
    above = lax.rem(ring + 1, faces * tiles)
    below = lax.rem(ring + faces * tiles - 1, faces * tiles)
    above = (lax.div(above, tiles), lax.rem(above, tiles))
    below = (lax.div(below, tiles), lax.rem(below, tiles))
    others = [(lax.rem(face + d, faces), tile) for d in range(1, faces)]
    odd = lax.rem(lax.div(face, 2), 2)
    swap = 1 - 2 * lax.rem(face, 2)

    barrier = pltpu.get_barrier_semaphore()
    for partner in others + [above, below]:
        pl.semaphore_signal(barrier, inc=1, device_id=partner, device_id_type=MESH)

    loads = [
        pltpu.make_async_copy(src, dst, in_sem.at[n])
        for n, (src, dst) in enumerate(
            [
                (owner_hbm, owner_in),
                (forcing_hbm, x_in),
                (mask_hbm, mask_in),
                (vel_hbm, vel_in),
                (strength_hbm, strength_in),
                (mass_hbm, mass_in),
            ]
        )
    ]
    for load in loads:
        load.start()

    row128 = iota((128, 128), 0)
    lane128 = iota((128, 128), 1)
    eye = row128 == lane128
    ones = jnp.ones((128, 128), BF16)
    mirror = (row128 + lane128 == 127).astype(F32).astype(BF16)
    loads[0].wait()
    owner = owner_in[...]
    owner_lanes = jnp.broadcast_to(owner, (128, 128))
    owner_rows = dot(jnp.where(eye, owner_lanes.astype(F32), 0.0).astype(BF16), ones)
    same = (owner_rows == owner_lanes.astype(F32)) & (row128 <= lane128)
    rank = jnp.sum(same.astype(F32), axis=0, keepdims=True) - 1.0
    owner_odd = (owner & 2) == 2
    rank = jnp.where(owner_odd, 7.0 - rank, rank)
    place = owner.astype(F32) * 8.0 + rank
    place_lanes = jnp.broadcast_to(place, (128, 128))
    sorter = jnp.where(row128.astype(F32) == place_lanes, 1.0, 0.0)
    slot_odd = (row128 & 16) == 16
    sorter = jnp.concatenate(
        [jnp.where(slot_odd, 0.0, sorter), jnp.where(slot_odd, sorter, 0.0)], axis=1
    ).astype(BF16)
    loads[1].wait()
    x = x_in[...]
    spread[0:512, :] = x.astype(F32)
    sign_x = jnp.where((iota((512, 128), 0) & 1) == 0, -1.0, 1.0)
    spread[512:1024, :] = dot(x, mirror) * sign_x
    wide = jnp.concatenate(
        [
            jnp.concatenate(
                [spread[pl.ds(512 * n + c, 128, stride=4), :].astype(BF16) for c in range(4)],
                axis=1,
            )
            for n in range(2)
        ],
        axis=0,
    )
    grouped = dot(sorter, wide)
    for g in range(16):
        send_f[32 * g : 32 * g + 32, :] = jnp.concatenate(
            [grouped[8 * g : 8 * g + 8, 128 * c : 128 * c + 128] for c in range(4)], axis=0
        ).astype(BF16)

    def landing(odd_there):
        return face + odd_there * swap

    pl.semaphore_wait(barrier, faces + 1)

    def forcing_copy(d):
        g = others[d - 1][0]
        there = landing(lax.rem(lax.div(g, 2), 2))
        return pltpu.make_async_remote_copy(
            src_ref=send_f.at[pl.ds(pl.multiple_of(g * 32, 32), 32), :],
            dst_ref=f_all.at[pl.ds(pl.multiple_of(512 + there * 32, 32), 32), :],
            send_sem=f_send.at[d - 1],
            recv_sem=f_recv.at[d - 1],
            device_id=others[d - 1],
            device_id_type=MESH,
        )

    forcing_copies = [forcing_copy(d) for d in range(1, 16)]
    for copy in forcing_copies:
        copy.start()
    f_all[pl.ds(pl.multiple_of(512 + landing(odd) * 32, 32), 32), :] = send_f[
        pl.ds(pl.multiple_of(face * 32, 32), 32), :
    ]

    loads[2].wait()
    mask_lanes = jnp.broadcast_to(mask_in[...].astype(F32), (128, 128))
    flipped = row128 ^ (odd * 15)
    cover = dot(jnp.where(flipped == lane128, mask_lanes, 0.0).astype(BF16), ones)
    for load in loads[3:]:
        load.wait()

    def stage(mirrored):
        for b in range(ROW):
            spot = pl.ds(OWN + (ROW - 1 - b if mirrored else b), 8, stride=ROW)
            cols = slice(128 * b, 128 * b + 128)
            turned = flip_lanes if mirrored else (lambda value: value)
            u = turned(vel_in[0, :, cols])
            u1[spot, :] = -u if mirrored else u
            v1[spot, :] = turned(vel_in[1, :, cols])
            p_all[spot, :] = turned(strength_in[:, cols])
            m_all[spot, :] = turned(mass_in[:, cols])

    @pl.when(odd == 0)
    def _():
        stage(False)

    @pl.when(odd == 1)
    def _():
        stage(True)

    p_all[OWN : OWN + 128, :] = p_all[OWN : OWN + 128, :] * cover * F32(1.0 / 3.0)

    def halo_copies(pairs, send_sem, recv_sem):
        out = []
        for n, (src, dst, up, down) in enumerate(pairs):
            for way, ((lo, hi), there) in enumerate([(up, above), (down, below)]):
                shift = -128 if way == 0 else 128
                out.append(
                    pltpu.make_async_remote_copy(
                        src_ref=src.at[OWN + ROW * lo : OWN + ROW * hi, :],
                        dst_ref=dst.at[OWN + shift + ROW * lo : OWN + shift + ROW * hi, :],
                        send_sem=send_sem.at[2 * n + way],
                        recv_sem=recv_sem.at[2 * n + way],
                        device_id=there,
                        device_id_type=MESH,
                    )
                )
        return out

    first_halo = halo_copies(
        [
            (u1, u1, (0, 8), (0, 8)),
            (v1, v1, (0, 8), (0, 8)),
            (p_all, p_all, (1, 8), (0, 7)),
            (m_all, m_all, (2, 8), (0, 6)),
        ],
        h_send,
        h_recv,
    )
    for copy in first_halo:
        copy.start()

    place_rows = dot(jnp.where(eye, place_lanes, 0.0).astype(BF16), ones)
    unsort[...] = jnp.where(place_rows == lane128.astype(F32), 1.0, 0.0).astype(BF16)
    for ref in (a1, a2, a12):
        ref[...] = jnp.zeros_like(ref)

    for copy in forcing_copies:
        copy.wait_recv()
    forcing_halo = [
        pltpu.make_async_remote_copy(
            src_ref=f_all.at[512 + 64 * lo : 512 + 64 * lo + 384, :],
            dst_ref=f_all.at[512 + shift + 64 * lo : 512 + shift + 64 * lo + 384, :],
            send_sem=g_send.at[way],
            recv_sem=g_recv.at[way],
            device_id=there,
            device_id_type=MESH,
        )
        for way, (lo, shift, there) in enumerate([(2, -512, above), (0, 512, below)])
    ]
    for copy in forcing_halo:
        copy.start()
    for copy in first_halo:
        copy.wait_recv()
    for copy in forcing_halo:
        copy.wait_recv()
    for copy in forcing_copies + first_halo + forcing_halo:
        copy.wait_send()

    cor = [
        0.5 - lax.rem(lax.div(f, 2), 2).astype(F32) for f in (below[0], face, above[0])
    ]
    subcycles(cor, u1, v1, (a1, a2, a12), p_all, m_all, f_all)
    mid_halo = halo_copies(
        [
            (u1, u2, (0, 8), (0, 8)),
            (v1, v2, (0, 8), (0, 8)),
            (a1, b1, (1, 8), (0, 7)),
            (a2, b2, (1, 8), (0, 7)),
            (a12, b12, (1, 8), (0, 7)),
        ],
        k_send,
        k_recv,
    )
    for copy in mid_halo:
        copy.start()
    for src, dst in ((u1, u2), (v1, v2), (a1, b1), (a2, b2), (a12, b12)):
        dst[OWN : OWN + 128, :] = src[OWN : OWN + 128, :]
    for copy in mid_halo:
        copy.wait_recv()
    for copy in mid_halo:
        copy.wait_send()
    subcycles(cor, u2, v2, (b1, b2, b12), p_all, m_all, f_all)

    turn = jnp.where(odd == 1, (row128 + lane128 == 127).astype(F32), eye.astype(F32)).astype(BF16)
    sign_u = (1 - 2 * odd).astype(F32)
    for i in range(8):
        uo, vo, _, _ = forcing_row(f_all, 8 + i)
        (u,), (v,), (p,) = (rows_of(ref, 8 + i, 1) for ref in (u2, v2, p_all))
        du = u - uo
        dv = v - vo
        speed = jnp.where(p > 0.0, jnp.sqrt(du * du + dv * dv), 0.0)
        du = sign_u * (speed * du)
        dv = speed * dv
        both = jnp.concatenate([du[0:8], dv[0:8], du[8:16], dv[8:16]], axis=0).astype(BF16)
        send_d[32 * i : 32 * i + 32, :] = dot(both, turn).astype(BF16)

    def drag_copy(d):
        g = others[d - 1][0]
        from_here = g + odd * (1 - 2 * lax.rem(g, 2))
        return pltpu.make_async_remote_copy(
            src_ref=send_d.at[pl.ds(pl.multiple_of(from_here * 16, 16), 16), :],
            dst_ref=recv_d.at[pl.ds(pl.multiple_of(face * 16, 16), 16), :],
            send_sem=d_send.at[d - 1],
            recv_sem=d_recv.at[d - 1],
            device_id=others[d - 1],
            device_id_type=MESH,
        )

    drag_copies = [drag_copy(d) for d in range(1, 16)]
    for copy in drag_copies:
        copy.start()
    recv_d[pl.ds(pl.multiple_of(face * 16, 16), 16), :] = send_d[
        pl.ds(pl.multiple_of(landing(odd) * 16, 16), 16), :
    ]

    def finish(mirrored):
        for b in range(ROW):
            spot = pl.ds(OWN + (ROW - 1 - b if mirrored else b), 8, stride=ROW)
            cols = slice(128 * b, 128 * b + 128)
            u = u2[spot, :]
            v = v2[spot, :]
            vel_buf[0, :, cols] = -flip_lanes(u) if mirrored else u
            vel_buf[1, :, cols] = flip_lanes(v) if mirrored else v

    @pl.when(odd == 0)
    def _():
        finish(False)

    @pl.when(odd == 1)
    def _():
        finish(True)

    vel_store = pltpu.make_async_copy(vel_buf, vel_out, out_sem.at[0])
    vel_store.start()

    for copy in drag_copies:
        copy.wait_recv()
    back = recv_d[...].astype(F32)
    for c in range(2):
        part = jnp.concatenate(
            [back[16 * g + 8 * c : 16 * g + 8 * c + 8] for g in range(16)], axis=0
        ).astype(BF16)
        unsorted[pl.ds(c, 128, stride=2), :] = dot(unsort[...], part)
    drag_buf[...] = unsorted[...].astype(BF16)
    drag_store = pltpu.make_async_copy(drag_buf, drag_out, out_sem.at[1])
    drag_store.start()
    for copy in drag_copies:
        copy.wait_send()
    vel_store.wait()
    drag_store.wait()


def per_device(ocean_forcing, ice_owner, ice_mask, ice_velocity, ice_mass, ice_strength):
    field = pltpu.VMEM((24 * ROW, 128), F32)
    dma = pltpu.SemaphoreType.DMA
    velocity, drag = pl.pallas_call(
        kernel,
        out_shape=(
            jax.ShapeDtypeStruct((2, 8, 2048), F32),
            jax.ShapeDtypeStruct((256, 128), BF16),
        ),
        in_specs=[pl.BlockSpec(memory_space=pl.ANY)] * 6,
        out_specs=(pl.BlockSpec(memory_space=pl.ANY), pl.BlockSpec(memory_space=pl.ANY)),
        scratch_shapes=[
            pltpu.VMEM((512, 128), BF16),
            pltpu.VMEM((1, 128), jnp.int32),
            pltpu.VMEM((1, 128), jnp.int32),
            pltpu.VMEM((2, 8, 2048), F32),
            pltpu.VMEM((8, 2048), F32),
            pltpu.VMEM((8, 2048), F32),
            pltpu.VMEM((1024, 128), F32),
            pltpu.VMEM((512, 128), BF16),
            pltpu.VMEM((1536, 128), BF16),
        ]
        + [field] * 12
        + [
            pltpu.VMEM((256, 128), BF16),
            pltpu.VMEM((256, 128), BF16),
            pltpu.VMEM((128, 128), BF16),
            pltpu.VMEM((256, 128), F32),
            pltpu.VMEM((256, 128), BF16),
            pltpu.VMEM((2, 8, 2048), F32),
            dma((6,)),
            dma((2,)),
            dma((15,)),
            dma((15,)),
            dma((8,)),
            dma((8,)),
            dma((2,)),
            dma((2,)),
            dma((10,)),
            dma((10,)),
            dma((15,)),
            dma((15,)),
        ],
        compiler_params=pltpu.CompilerParams(
            collective_id=0, has_side_effects=True, vmem_limit_bytes=32 * 2**20
        ),
    )(
        ocean_forcing.reshape(512, 128),
        ice_owner,
        ice_mask,
        ice_velocity.reshape(2, 8, 2048),
        ice_mass.reshape(8, 2048),
        ice_strength.reshape(8, 2048),
    )
    return velocity.reshape(2, 1, 8, 2048), drag.reshape(1, 128, 2, 128)


def solution(mesh):
    in_specs = (
        P("face", "tile", None, None),
        P("face", "tile"),
        P("face", "tile"),
        P(None, "face", "tile", None),
        P("face", "tile", None),
        P("face", "tile", None),
    )
    out_specs = (P(None, "face", "tile", None), P("face", "tile", None, None))
    return jax.shard_map(
        per_device, mesh=mesh, in_specs=in_specs, out_specs=out_specs, check_vma=False
    )
```

```python
import jax
import jax.numpy as jnp
from jax import lax
from jax.experimental import pallas as pl
from jax.experimental.pallas import tpu as pltpu
from jax.sharding import PartitionSpec as P

MESH = pl.DeviceIdType.MESH
F32 = jnp.float32
BF16 = jnp.bfloat16
ROW = 16
OWN = 8 * ROW
F_OWN = 512


def iota(shape, dim):
    return lax.broadcasted_iota(jnp.int32, shape, dim)


def dot(a, b):
    return jnp.dot(a, b, preferred_element_type=F32)


def flip_lanes(x):
    return jnp.take_along_axis(x, 127 - iota(x.shape, 1), axis=1)


def centred_x(x):
    lane = iota(x.shape, 1)
    ahead = pltpu.roll(x, 127, 1)
    behind = pltpu.roll(x, 1, 1)
    ahead = jnp.where(lane == 127, pltpu.roll(ahead, ROW - 1, 0), ahead)
    behind = jnp.where(lane == 0, pltpu.roll(behind, 1, 0), behind)
    return ahead - behind


def rows_of(ref, first, count):
    return [ref[pl.ds(pl.multiple_of((first + n) * ROW, ROW), ROW), :] for n in range(count)]


def put_row(ref, row, value):
    ref[pl.ds(pl.multiple_of(row * ROW, ROW), ROW), :] = value


def stress_rows(first, count, u_ref, v_ref, stress, p_ref):
    us = rows_of(u_ref, first - 1, count + 2)
    vs = rows_of(v_ref, first - 1, count + 2)
    ps = rows_of(p_ref, first, count)
    old = [rows_of(s, first, count) for s in stress]
    third = F32(2.0 / 3.0)
    for n in range(count):
        e11 = centred_x(us[n + 1])
        e22 = vs[n + 2] - vs[n]
        shear = (us[n + 2] - us[n]) + centred_x(vs[n + 1])
        dd = e11 + e22
        dtn = e11 - e22
        inv = lax.rsqrt(dd * dd + 0.25 * (dtn * dtn + shear * shear) + 0.04)
        grip = ps[n] * inv
        put_row(stress[0], first + n, third * old[0][n] + (grip * dd - ps[n]))
        put_row(stress[1], first + n, third * old[1][n] + 0.25 * (grip * dtn))
        put_row(stress[2], first + n, third * old[2][n] + 0.125 * (grip * shear))


def forcing_row(f_ref, row):
    block = f_ref[pl.ds(pl.multiple_of(row * 64, 64), 64), :].astype(F32)
    return [
        jnp.concatenate([block[8 * c : 8 * c + 8], block[32 + 8 * c : 40 + 8 * c]], axis=0)
        for c in range(4)
    ]


def momentum_rows(first, count, cor, u_ref, v_ref, stress, p_ref, m_ref, f_ref):
    s1 = rows_of(stress[0], first - 1, count + 2)
    s2 = rows_of(stress[1], first - 1, count + 2)
    s12 = rows_of(stress[2], first - 1, count + 2)
    us = rows_of(u_ref, first, count)
    vs = rows_of(v_ref, first, count)
    ps = rows_of(p_ref, first, count)
    ms = rows_of(m_ref, first, count)
    for n in range(count):
        uo, vo, tx, ty = forcing_row(f_ref, first + n)
        u, v, m = us[n], vs[n], ms[n]
        fx = 0.25 * centred_x(s1[n + 1] + s2[n + 1]) + 0.5 * (s12[n + 2] - s12[n])
        fy = 0.5 * centred_x(s12[n + 1]) + 0.25 * ((s1[n + 2] - s2[n + 2]) - (s1[n] - s2[n]))
        du = uo - u
        dv = vo - v
        speed = jnp.sqrt(du * du + dv * dv)
        row = first + n
        sign = jnp.where(row < 8, cor[0], jnp.where(row < 16, cor[1], cor[2]))
        turn = sign * m
        inv = jnp.where(ps[n] > 0.0, 1.0 / (m + 0.25 * speed), 0.0)
        put_row(u_ref, first + n, (m * u + 0.25 * (fx + tx + speed * uo + turn * v)) * inv)
        put_row(v_ref, first + n, (m * v + 0.25 * (fy + ty + speed * vo - turn * u)) * inv)


def kernel(
    forcing_hbm, owner_hbm, mask_hbm, vel_hbm, mass_hbm, strength_hbm,
    vel_out, drag_out,
    x_in, owner_in, mask_in, vel_in, mass_in, strength_in,
    spread, send_f, f_all, u_all, v_all, p_all, m_all, a1, a2, a12,
    mid_out, mid_in, send_d, recv_d, unsort, unsorted,
    in_sem, f_send, f_recv, h_send, h_recv, g_send, g_recv,
    k_send, k_recv, d_send, d_recv, edge,
):
    face = lax.axis_index("face")
    tile = lax.axis_index("tile")
    faces = lax.axis_size("face")
    tiles = lax.axis_size("tile")
    ring = face * tiles + tile

    def along(step):
        there = lax.rem(ring + step + faces * tiles, faces * tiles)
        return lax.div(there, tiles), lax.rem(there, tiles)

    above, below = along(1), along(-1)
    chip = lax.div(face, 2)
    odd = lax.rem(chip, 2)
    swap = 1 - 2 * lax.rem(face, 2)
    first = tile == 0
    last = tile == tiles - 1

    def other(n):
        half = lax.div(n + 1, 2)
        return lax.rem(face + 8 + jnp.where(lax.rem(n, 2) == 0, half, -half), faces)

    def remote(src, dst, send_sem, recv_sem, there):
        return pltpu.make_async_remote_copy(
            src_ref=src,
            dst_ref=dst,
            send_sem=send_sem,
            recv_sem=recv_sem,
            device_id=there,
            device_id_type=MESH,
        )

    def rows_at(ref, start, size):
        return ref.at[pl.ds(pl.multiple_of(start, 16), size), :]

    loads = [
        pltpu.make_async_copy(src, dst, in_sem.at[n])
        for n, (src, dst) in enumerate(
            [
                (owner_hbm, owner_in),
                (forcing_hbm, x_in),
                (mask_hbm, mask_in),
                (vel_hbm, vel_in),
                (strength_hbm, strength_in),
                (mass_hbm, mass_in),
            ]
        )
    ]
    for load in loads:
        load.start()

    barrier = pltpu.get_barrier_semaphore()

    def greet(there):
        pl.semaphore_signal(barrier, inc=1, device_id=there, device_id_type=MESH)

    def greet_face(n, carry):
        greet((other(n), tile))
        return carry

    lax.fori_loop(0, 15, greet_face, 0)
    greet(below)

    @pl.when(jnp.logical_not(last))
    def _():
        greet(above)

    row128 = iota((128, 128), 0)
    lane128 = iota((128, 128), 1)
    eye = row128 == lane128
    ones = jnp.ones((128, 128), BF16)
    mirror = (row128 + lane128 == 127).astype(F32).astype(BF16)
    loads[0].wait()
    owner = owner_in[...]
    owner_lanes = jnp.broadcast_to(owner, (128, 128))
    owner_rows = dot(jnp.where(eye, owner_lanes.astype(F32), 0.0).astype(BF16), ones)
    same = (owner_rows == owner_lanes.astype(F32)) & (row128 <= lane128)
    rank = jnp.sum(same.astype(F32), axis=0, keepdims=True) - 1.0
    owner_odd = (owner & 2) == 2
    rank = jnp.where(owner_odd, 7.0 - rank, rank)
    place = owner.astype(F32) * 8.0 + rank
    place_lanes = jnp.broadcast_to(place, (128, 128))
    sorter = jnp.where(row128.astype(F32) == place_lanes, 1.0, 0.0)
    slot_odd = (row128 & 16) == 16
    sorter = jnp.concatenate(
        [jnp.where(slot_odd, 0.0, sorter), jnp.where(slot_odd, sorter, 0.0)], axis=1
    ).astype(BF16)
    loads[1].wait()
    x = x_in[...]
    spread[0:512, :] = x.astype(F32)
    sign_x = jnp.where((iota((512, 128), 0) & 1) == 0, -1.0, 1.0)
    spread[512:1024, :] = dot(x, mirror) * sign_x
    wide = jnp.concatenate(
        [
            jnp.concatenate(
                [spread[pl.ds(512 * n + c, 128, stride=4), :].astype(BF16) for c in range(4)],
                axis=1,
            )
            for n in range(2)
        ],
        axis=0,
    )
    grouped = dot(sorter, wide)
    for g in range(16):
        send_f[32 * g : 32 * g + 32, :] = jnp.concatenate(
            [grouped[8 * g : 8 * g + 8, 128 * c : 128 * c + 128] for c in range(4)], axis=0
        ).astype(BF16)

    def landing(f, odd_there):
        return f + odd_there * (1 - 2 * lax.rem(f, 2))

    pl.semaphore_wait(barrier, faces + jnp.minimum(tile, 1))

    def forcing_copy(n):
        g = other(n)
        there = landing(face, lax.rem(lax.div(g, 2), 2))
        return remote(
            rows_at(send_f, g * 32, 32),
            rows_at(f_all, F_OWN + there * 32, 32),
            f_send.at[n],
            f_recv.at[face],
            (g, tile),
        )

    def forcing_start(n, carry):
        forcing_copy(n).start()
        return carry

    lax.fori_loop(0, 15, forcing_start, 0)

    @pl.when(last)
    def _():
        pl.semaphore_signal(edge, inc=1, device_id=above, device_id_type=MESH)

    f_all[pl.ds(pl.multiple_of(F_OWN + landing(face, odd) * 32, 32), 32), :] = send_f[
        pl.ds(pl.multiple_of(face * 32, 32), 32), :
    ]

    loads[2].wait()
    mask_lanes = jnp.broadcast_to(mask_in[...].astype(F32), (128, 128))
    flipped = row128 ^ (odd * 15)
    cover = dot(jnp.where(flipped == lane128, mask_lanes, 0.0).astype(BF16), ones)
    for load in loads[3:]:
        load.wait()

    def stage(mirrored):
        for b in range(ROW):
            spot = pl.ds(OWN + (ROW - 1 - b if mirrored else b), 8, stride=ROW)
            cols = slice(128 * b, 128 * b + 128)
            turned = flip_lanes if mirrored else (lambda value: value)
            u = turned(vel_in[0, :, cols])
            u_all[spot, :] = -u if mirrored else u
            v_all[spot, :] = turned(vel_in[1, :, cols])
            p_all[spot, :] = turned(strength_in[:, cols])
            m_all[spot, :] = turned(mass_in[:, cols])

    @pl.when(odd == 0)
    def _():
        stage(False)

    @pl.when(odd == 1)
    def _():
        stage(True)

    mine = slice(OWN, OWN + 128)
    p_all[mine, :] = p_all[mine, :] * cover * F32(1.0 / 3.0)

    state = (u_all, v_all, p_all, m_all)

    def state_copies(shift, way, there, send_sem, recv_sem):
        return [
            remote(
                ref.at[OWN : OWN + 128, :],
                ref.at[OWN + shift : OWN + shift + 128, :],
                send_sem.at[2 * n + way],
                recv_sem.at[2 * n + way],
                there,
            )
            for n, ref in enumerate(state)
        ]

    near_up = state_copies(-128, 0, above, h_send, h_recv)
    near_down = state_copies(128, 1, below, h_send, h_recv)

    def start(copies):
        for copy in copies:
            copy.start()

    start(near_up)

    @pl.when(jnp.logical_not(first))
    def _():
        start(near_down)

    place_rows = dot(jnp.where(eye, place_lanes, 0.0).astype(BF16), ones)
    unsort[...] = jnp.where(place_rows == lane128.astype(F32), 1.0, 0.0).astype(BF16)
    for ref in (a1, a2, a12):
        ref[...] = jnp.zeros_like(ref)

    def forcing_row_copy(start, size, way):
        shift = 512 if way else -512
        return remote(
            rows_at(f_all, F_OWN + start, size),
            rows_at(f_all, F_OWN + shift + start, size),
            g_send.at[way],
            g_recv.at[way],
            below if way else above,
        )

    def arrived(f):
        place = landing(f, odd)
        remote(
            rows_at(send_f, 0, 32),
            rows_at(f_all, F_OWN + place * 32, 32),
            f_send.at[0],
            f_recv.at[f],
            above,
        ).wait_recv()

    def pass_row(n, carry):
        step = jnp.where(lax.rem(n, 2) == 1, lax.div(n + 1, 2), 8 - lax.div(n, 2))
        row = lax.rem(chip + step, 8)

        @pl.when(n == 0)
        def _():
            arrived(face + swap)

        @pl.when(n > 0)
        def _():
            arrived(2 * row)
            arrived(2 * row + 1)

        @pl.when(row >= 2)
        def _():
            forcing_row_copy(row * 64, 64, 0).start()

        @pl.when((row < 6) & jnp.logical_not(first))
        def _():
            forcing_row_copy(row * 64, 64, 1).start()

        return carry

    lax.fori_loop(0, 8, pass_row, 0)

    @pl.when(first)
    def _():
        pl.semaphore_wait(edge, 1)
        start(near_down)
        forcing_row_copy(0, 384, 1).start()

    forcing_halo = [forcing_row_copy(128, 384, 0), forcing_row_copy(0, 384, 1)]
    for copy in near_up + near_down + forcing_halo:
        copy.wait_recv()
    for copy in near_up + near_down + forcing_halo:
        copy.wait_send()

    stress = (a1, a2, a12)
    moving = (u_all, v_all, a1, a2, a12)

    def mid_copies(way):
        there = below if way else above
        out = []
        for n in range(5):
            lo, hi = (0, 128) if n < 2 else ((0, 112) if way else (16, 128))
            out.append(
                remote(
                    mid_out.at[n, lo:hi, :],
                    mid_in.at[way, n, lo:hi, :],
                    k_send.at[2 * n + way],
                    k_recv.at[2 * n + way],
                    there,
                )
            )
        return out

    mid_up, mid_down = mid_copies(0), mid_copies(1)

    def middle():
        for n, ref in enumerate(moving):
            mid_out[n] = ref[mine, :]
        start(mid_up + mid_down)
        for copy in mid_up + mid_down:
            copy.wait_recv()
        for n, ref in enumerate(moving):
            lo, hi = (0, 128) if n < 2 else (16, 128)
            ref[OWN - 128 + lo : OWN - 128 + hi, :] = mid_in[0, n, lo:hi, :]
            lo, hi = (0, 128) if n < 2 else (0, 112)
            ref[OWN + 128 + lo : OWN + 128 + hi, :] = mid_in[1, n, lo:hi, :]

    cor = [
        0.5 - lax.rem(lax.div(f, 2), 2).astype(F32)
        for f in (below[0], face, above[0])
    ]

    def cycle(k, carry):
        reach = 7 - 2 * lax.rem(k, 4)
        top = 8 - reach
        bodies = lax.div(reach + 3, 2)

        @pl.when(k == 4)
        def _():
            middle()

        def stress_part(n, c):
            stress_rows(top + 4 * n, 4, u_all, v_all, stress, p_all)
            return c

        def momentum_part(n, c):
            momentum_rows(top + 1 + 4 * n, 4, cor, u_all, v_all, stress, p_all, m_all, f_all)
            return c

        lax.fori_loop(0, bodies, stress_part, 0)
        stress_rows(top + 4 * bodies, 2, u_all, v_all, stress, p_all)
        lax.fori_loop(0, bodies, momentum_part, 0)
        return carry

    lax.fori_loop(0, 8, cycle, 0)

    turn = jnp.where(odd == 1, (row128 + lane128 == 127).astype(F32), eye.astype(F32)).astype(BF16)
    sign_u = (1 - 2 * odd).astype(F32)
    for i in range(8):
        uo, vo, _, _ = forcing_row(f_all, 8 + i)
        (u,), (v,), (p,) = (rows_of(ref, 8 + i, 1) for ref in (u_all, v_all, p_all))
        du = u - uo
        dv = v - vo
        speed = jnp.where(p > 0.0, jnp.sqrt(du * du + dv * dv), 0.0)
        du = sign_u * (speed * du)
        dv = speed * dv
        both = jnp.concatenate([du[0:8], dv[0:8], du[8:16], dv[8:16]], axis=0).astype(BF16)
        send_d[32 * i : 32 * i + 32, :] = dot(both, turn).astype(BF16)

    def drag_copy(n):
        g = other(n)
        return remote(
            rows_at(send_d, landing(g, odd) * 16, 16),
            rows_at(recv_d, face * 16, 16),
            d_send.at[n],
            d_recv.at[n],
            (g, tile),
        )

    def drag_start(n, carry):
        drag_copy(n).start()
        return carry

    lax.fori_loop(0, 15, drag_start, 0)
    recv_d[pl.ds(pl.multiple_of(face * 16, 16), 16), :] = send_d[
        pl.ds(pl.multiple_of(landing(face, odd) * 16, 16), 16), :
    ]

    def finish(mirrored):
        for b in range(ROW):
            spot = pl.ds(OWN + (ROW - 1 - b if mirrored else b), 8, stride=ROW)
            cols = slice(128 * b, 128 * b + 128)
            u = u_all[spot, :]
            v = v_all[spot, :]
            vel_out[0, :, cols] = -flip_lanes(u) if mirrored else u
            vel_out[1, :, cols] = flip_lanes(v) if mirrored else v

    @pl.when(odd == 0)
    def _():
        finish(False)

    @pl.when(odd == 1)
    def _():
        finish(True)

    def sent(n, carry):
        forcing_copy(n).wait_send()
        return carry

    lax.fori_loop(0, 15, sent, 0)

    for copy in mid_up + mid_down:
        copy.wait_send()

    def returned(n, carry):
        drag_copy(n).wait()
        return carry

    lax.fori_loop(0, 15, returned, 0)
    back = recv_d[...].astype(F32)
    for c in range(2):
        part = jnp.concatenate(
            [back[16 * g + 8 * c : 16 * g + 8 * c + 8] for g in range(16)], axis=0
        ).astype(BF16)
        unsorted[pl.ds(c, 128, stride=2), :] = dot(unsort[...], part)
    drag_out[...] = unsorted[...].astype(BF16)


def per_device(ocean_forcing, ice_owner, ice_mask, ice_velocity, ice_mass, ice_strength):
    field = pltpu.VMEM((24 * ROW, 128), F32)
    dma = pltpu.SemaphoreType.DMA
    velocity, drag = pl.pallas_call(
        kernel,
        out_shape=(pltpu.VMEM((2, 8, 2048), F32), pltpu.VMEM((256, 128), BF16)),
        in_specs=[pl.BlockSpec(memory_space=pl.ANY)] * 6,
        out_specs=[pl.BlockSpec(memory_space=pltpu.VMEM)] * 2,
        scratch_shapes=[
            pltpu.VMEM((512, 128), BF16),
            pltpu.VMEM((1, 128), jnp.int32),
            pltpu.VMEM((1, 128), jnp.int32),
            pltpu.VMEM((2, 8, 2048), F32),
            pltpu.VMEM((8, 2048), F32),
            pltpu.VMEM((8, 2048), F32),
            pltpu.VMEM((1024, 128), F32),
            pltpu.VMEM((512, 128), BF16),
            pltpu.VMEM((3 * 512, 128), BF16),
        ]
        + [field] * 7
        + [
            pltpu.VMEM((5, 128, 128), F32),
            pltpu.VMEM((2, 5, 128, 128), F32),
            pltpu.VMEM((256, 128), BF16),
            pltpu.VMEM((256, 128), BF16),
            pltpu.VMEM((128, 128), BF16),
            pltpu.VMEM((256, 128), F32),
            dma((6,)),
            dma((15,)),
            dma((16,)),
            dma((8,)),
            dma((8,)),
            dma((2,)),
            dma((2,)),
            dma((10,)),
            dma((10,)),
            dma((15,)),
            dma((15,)),
            pltpu.SemaphoreType.REGULAR,
        ],
        compiler_params=pltpu.CompilerParams(
            collective_id=0, has_side_effects=True, vmem_limit_bytes=60 * 2**20
        ),
    )(
        ocean_forcing.reshape(512, 128),
        ice_owner,
        ice_mask,
        ice_velocity.reshape(2, 8, 2048),
        ice_mass.reshape(8, 2048),
        ice_strength.reshape(8, 2048),
    )
    return velocity.reshape(2, 1, 8, 2048), drag.reshape(1, 128, 2, 128)


def solution(mesh):
    in_specs = (
        P("face", "tile", None, None),
        P("face", "tile"),
        P("face", "tile"),
        P(None, "face", "tile", None),
        P("face", "tile", None),
        P("face", "tile", None),
    )
    out_specs = (P(None, "face", "tile", None), P("face", "tile", None, None))
    return jax.shard_map(
        per_device, mesh=mesh, in_specs=in_specs, out_specs=out_specs, check_vma=False
    )
```

```python
import jax
import jax.numpy as jnp
from jax import lax
from jax.experimental import pallas as pl
from jax.experimental.pallas import tpu as pltpu
from jax.sharding import PartitionSpec as P

MESH = pl.DeviceIdType.MESH
F32 = jnp.float32
BF16 = jnp.bfloat16
ROW = 16
OWN = 9 * ROW
F_OWN = 512


def iota(shape, dim):
    return lax.broadcasted_iota(jnp.int32, shape, dim)


def dot(a, b):
    return jnp.dot(a, b, preferred_element_type=F32)


def flip_lanes(x):
    return jnp.take_along_axis(x, 127 - iota(x.shape, 1), axis=1)


def centred_x(x):
    lane = iota(x.shape, 1)
    ahead = pltpu.roll(x, 127, 1)
    behind = pltpu.roll(x, 1, 1)
    ahead = jnp.where(lane == 127, pltpu.roll(ahead, ROW - 1, 0), ahead)
    behind = jnp.where(lane == 0, pltpu.roll(behind, 1, 0), behind)
    return ahead - behind


def rows_of(ref, first, count):
    return [ref[(first + n) * ROW : (first + n + 1) * ROW, :] for n in range(count)]


def put_row(ref, row, value):
    ref[row * ROW : (row + 1) * ROW, :] = value


def stress_rows(first, count, u_ref, v_ref, stress, p_ref):
    us = rows_of(u_ref, first - 1, count + 2)
    vs = rows_of(v_ref, first - 1, count + 2)
    ps = rows_of(p_ref, first, count)
    old = [rows_of(s, first, count) for s in stress]
    third = F32(2.0 / 3.0)
    for n in range(count):
        e11 = centred_x(us[n + 1])
        e22 = vs[n + 2] - vs[n]
        shear = (us[n + 2] - us[n]) + centred_x(vs[n + 1])
        dd = e11 + e22
        dtn = e11 - e22
        inv = lax.rsqrt(dd * dd + 0.25 * (dtn * dtn + shear * shear) + 0.04)
        grip = ps[n] * inv
        put_row(stress[0], first + n, third * old[0][n] + (grip * dd - ps[n]))
        put_row(stress[1], first + n, third * old[1][n] + 0.25 * (grip * dtn))
        put_row(stress[2], first + n, third * old[2][n] + 0.125 * (grip * shear))


def forcing_row(f_ref, row):
    block = f_ref[row * 64 : row * 64 + 64, :].astype(F32)
    return [
        jnp.concatenate([block[8 * c : 8 * c + 8], block[32 + 8 * c : 40 + 8 * c]], axis=0)
        for c in range(4)
    ]


def momentum_rows(first, count, cor, u_ref, v_ref, stress, p_ref, m_ref, f_ref):
    s1 = rows_of(stress[0], first - 1, count + 2)
    s2 = rows_of(stress[1], first - 1, count + 2)
    s12 = rows_of(stress[2], first - 1, count + 2)
    us = rows_of(u_ref, first, count)
    vs = rows_of(v_ref, first, count)
    ps = rows_of(p_ref, first, count)
    ms = rows_of(m_ref, first, count)
    for n in range(count):
        uo, vo, tx, ty = forcing_row(f_ref, first + n - 1)
        u, v, m = us[n], vs[n], ms[n]
        fx = 0.25 * centred_x(s1[n + 1] + s2[n + 1]) + 0.5 * (s12[n + 2] - s12[n])
        fy = 0.5 * centred_x(s12[n + 1]) + 0.25 * ((s1[n + 2] - s2[n + 2]) - (s1[n] - s2[n]))
        du = uo - u
        dv = vo - v
        speed = jnp.sqrt(du * du + dv * dv)
        row = first + n
        sign = cor[0] if row < 9 else cor[1] if row < 17 else cor[2]
        turn = sign * m
        inv = jnp.where(ps[n] > 0.0, 1.0 / (m + 0.25 * speed), 0.0)
        put_row(u_ref, first + n, (m * u + 0.25 * (fx + tx + speed * uo + turn * v)) * inv)
        put_row(v_ref, first + n, (m * v + 0.25 * (fy + ty + speed * vo - turn * u)) * inv)


def kernel(
    forcing_hbm, owner_hbm, mask_hbm, vel_hbm, mass_hbm, strength_hbm,
    vel_out, drag_out,
    x_in, owner_in, mask_in, vel_in, mass_in, strength_in,
    spread, send_f, f_all, u_all, v_all, p_all, m_all, a1, a2, a12,
    mid_out, mid_in, send_d, recv_d, unsort, unsorted,
    in_sem, f_send, f_recv, h_send, h_recv, g_send, g_recv,
    k_send, k_recv, d_send, d_recv, edge,
):
    face = lax.axis_index("face")
    tile = lax.axis_index("tile")
    faces = lax.axis_size("face")
    tiles = lax.axis_size("tile")
    ring = face * tiles + tile

    def along(step):
        there = lax.rem(ring + step + faces * tiles, faces * tiles)
        return lax.div(there, tiles), lax.rem(there, tiles)

    above, below = along(1), along(-1)
    chip = lax.div(face, 2)
    first = tile == 0
    last = tile == tiles - 1
    odd = lax.rem(chip, 2)
    swap = 1 - 2 * lax.rem(face, 2)

    def other(n):
        half = lax.div(n + 1, 2)
        return lax.rem(face + 8 + jnp.where(lax.rem(n, 2) == 0, half, -half), faces)

    def remote(src, dst, send_sem, recv_sem, there):
        return pltpu.make_async_remote_copy(
            src_ref=src,
            dst_ref=dst,
            send_sem=send_sem,
            recv_sem=recv_sem,
            device_id=there,
            device_id_type=MESH,
        )

    def rows_at(ref, start, size):
        return ref.at[pl.ds(pl.multiple_of(start, 16), size), :]

    loads = [
        pltpu.make_async_copy(src, dst, in_sem.at[n])
        for n, (src, dst) in enumerate(
            [
                (owner_hbm, owner_in),
                (forcing_hbm, x_in),
                (mask_hbm, mask_in),
                (vel_hbm, vel_in),
                (strength_hbm, strength_in),
                (mass_hbm, mass_in),
            ]
        )
    ]
    for load in loads:
        load.start()

    barrier = pltpu.get_barrier_semaphore()

    def greet(there):
        pl.semaphore_signal(barrier, inc=1, device_id=there, device_id_type=MESH)

    def greet_face(n, carry):
        greet((other(n), tile))
        return carry

    lax.fori_loop(0, 15, greet_face, 0)
    greet(below)

    @pl.when(jnp.logical_not(last))
    def _():
        greet(above)

    row128 = iota((128, 128), 0)
    lane128 = iota((128, 128), 1)
    eye = row128 == lane128
    ones = jnp.ones((128, 128), BF16)
    mirror = (row128 + lane128 == 127).astype(F32).astype(BF16)
    loads[0].wait()
    owner = owner_in[...]
    owner_lanes = jnp.broadcast_to(owner, (128, 128))
    owner_rows = dot(jnp.where(eye, owner_lanes.astype(F32), 0.0).astype(BF16), ones)
    same = (owner_rows == owner_lanes.astype(F32)) & (row128 <= lane128)
    rank = jnp.sum(same.astype(F32), axis=0, keepdims=True) - 1.0
    owner_odd = (owner & 2) == 2
    rank = jnp.where(owner_odd, 7.0 - rank, rank)
    place = owner.astype(F32) * 8.0 + rank
    place_lanes = jnp.broadcast_to(place, (128, 128))
    sorter = jnp.where(row128.astype(F32) == place_lanes, 1.0, 0.0)
    slot_odd = (row128 & 16) == 16
    sorter = jnp.concatenate(
        [jnp.where(slot_odd, 0.0, sorter), jnp.where(slot_odd, sorter, 0.0)], axis=1
    ).astype(BF16)
    loads[1].wait()
    x = x_in[...]
    spread[0:512, :] = x.astype(F32)
    sign_x = jnp.where((iota((512, 128), 0) & 1) == 0, -1.0, 1.0)
    spread[512:1024, :] = dot(x, mirror) * sign_x
    wide = jnp.concatenate(
        [
            jnp.concatenate(
                [spread[pl.ds(512 * n + c, 128, stride=4), :].astype(BF16) for c in range(4)],
                axis=1,
            )
            for n in range(2)
        ],
        axis=0,
    )
    grouped = dot(sorter, wide)
    for g in range(16):
        send_f[32 * g : 32 * g + 32, :] = jnp.concatenate(
            [grouped[8 * g : 8 * g + 8, 128 * c : 128 * c + 128] for c in range(4)], axis=0
        ).astype(BF16)

    loads[2].wait()
    mask_lanes = jnp.broadcast_to(mask_in[...].astype(F32), (128, 128))
    flipped = row128 ^ (odd * 15)
    cover = dot(jnp.where(flipped == lane128, mask_lanes, 0.0).astype(BF16), ones)
    for load in loads[3:]:
        load.wait()

    def stage(mirrored):
        for b in range(ROW):
            spot = pl.ds(OWN + (ROW - 1 - b if mirrored else b), 8, stride=ROW)
            cols = slice(128 * b, 128 * b + 128)
            turned = flip_lanes if mirrored else (lambda value: value)
            u = turned(vel_in[0, :, cols])
            u_all[spot, :] = -u if mirrored else u
            v_all[spot, :] = turned(vel_in[1, :, cols])
            p_all[spot, :] = turned(strength_in[:, cols])
            m_all[spot, :] = turned(mass_in[:, cols])

    @pl.when(odd == 0)
    def _():
        stage(False)

    @pl.when(odd == 1)
    def _():
        stage(True)

    mine = slice(OWN, OWN + 128)
    p_all[mine, :] = p_all[mine, :] * cover * F32(1.0 / 3.0)

    state = (u_all, v_all, p_all, m_all)

    def state_copies(shift, way, there, send_sem, recv_sem):
        lo = (0, 0, 0, 0) if way else (0, 0, 16, 32)
        hi = (128, 128, 112, 96) if way else (128, 128, 128, 128)
        return [
            remote(
                ref.at[OWN + lo[n] : OWN + hi[n], :],
                ref.at[OWN + shift + lo[n] : OWN + shift + hi[n], :],
                send_sem.at[2 * n + way],
                recv_sem.at[2 * n + way],
                there,
            )
            for n, ref in enumerate(state)
        ]

    near_up = state_copies(-128, 0, above, h_send, h_recv)
    near_down = state_copies(128, 1, below, h_send, h_recv)

    def start(copies):
        for copy in copies:
            copy.start()

    def landing(f, odd_there):
        return f + odd_there * (1 - 2 * lax.rem(f, 2))

    pl.semaphore_wait(barrier, 16 + jnp.minimum(tile, 1))

    @pl.when(last)
    def _():
        pl.semaphore_signal(edge, inc=1, device_id=above, device_id_type=MESH)

    start(near_up)

    @pl.when(jnp.logical_not(first))
    def _():
        start(near_down)


    def forcing_copy(n):
        g = other(n)
        there = landing(face, lax.rem(lax.div(g, 2), 2))
        return remote(
            rows_at(send_f, g * 32, 32),
            rows_at(f_all, F_OWN + there * 32, 32),
            f_send.at[n],
            f_recv.at[face],
            (g, tile),
        )

    def forcing_start(n, carry):
        forcing_copy(n).start()
        return carry

    lax.fori_loop(0, 15, forcing_start, 0)

    f_all[pl.ds(pl.multiple_of(F_OWN + landing(face, odd) * 32, 32), 32), :] = send_f[
        pl.ds(pl.multiple_of(face * 32, 32), 32), :
    ]

    place_rows = dot(jnp.where(eye, place_lanes, 0.0).astype(BF16), ones)
    unsort[...] = jnp.where(place_rows == lane128.astype(F32), 1.0, 0.0).astype(BF16)
    for ref in (a1, a2, a12):
        ref[...] = jnp.zeros_like(ref)

    def forcing_row_copy(start, size, way):
        shift = 512 if way else -512
        return remote(
            rows_at(f_all, F_OWN + start, size),
            rows_at(f_all, F_OWN + shift + start, size),
            g_send.at[way],
            g_recv.at[way],
            below if way else above,
        )

    def arrived(f):
        place = landing(f, odd)
        remote(
            rows_at(send_f, 0, 32),
            rows_at(f_all, F_OWN + place * 32, 32),
            f_send.at[0],
            f_recv.at[f],
            above,
        ).wait_recv()

    def pass_row(n, carry):
        step = jnp.where(lax.rem(n, 2) == 1, lax.div(n + 1, 2), 8 - lax.div(n, 2))
        row = lax.rem(chip + step, 8)

        @pl.when(n == 0)
        def _():
            arrived(face + swap)

        @pl.when(n > 0)
        def _():
            arrived(2 * row)
            arrived(2 * row + 1)

        @pl.when(row >= 2)
        def _():
            forcing_row_copy(row * 64, 64, 0).start()

        @pl.when((row < 6) & jnp.logical_not(first))
        def _():
            forcing_row_copy(row * 64, 64, 1).start()

        return carry

    lax.fori_loop(0, 8, pass_row, 0)

    @pl.when(first)
    def _():
        pl.semaphore_wait(edge, 1)
        start(near_down)
        forcing_row_copy(0, 384, 1).start()

    cor = [
        0.5 - lax.rem(lax.div(f, 2), 2).astype(F32) for f in (below[0], face, above[0])
    ]
    stress = (a1, a2, a12)

    def stresses(*parts):
        for lo, hi in parts:
            stress_rows(9 + lo, hi - lo, u_all, v_all, stress, p_all)

    def velocities(*parts):
        for lo, hi in parts:
            momentum_rows(9 + lo, hi - lo, cor, u_all, v_all, stress, p_all, m_all, f_all)

    for copy in near_up + near_down:
        copy.wait_recv()
    stresses((-7, 15))
    for copy in near_up + near_down:
        copy.wait_send()
    velocities((0, 8))
    stresses((1, 7))
    velocities((2, 6))
    stresses((3, 5))
    forcing_halo = [forcing_row_copy(128, 384, 0), forcing_row_copy(0, 384, 1)]
    for copy in forcing_halo:
        copy.wait_recv()
    velocities((-6, 0), (8, 14))
    stresses((-5, 1), (7, 13))
    velocities((-4, 2), (6, 12))
    stresses((-3, 3), (5, 11))
    velocities((-2, 10))
    stresses((-1, 9))
    velocities((0, 8))

    moving = (u_all, v_all, a1, a2, a12)

    def mid_copy(n, way):
        lo, hi = [((64, 128), (0, 64), (16, 64)), ((0, 64), (64, 128), (64, 112))][way][n]
        fields = (slice(0, 5), slice(0, 2), slice(2, 5))[n]
        return remote(
            mid_out.at[fields, lo:hi, :],
            mid_in.at[way, fields, lo:hi, :],
            k_send.at[2 * n + way],
            k_recv.at[2 * n + way],
            below if way else above,
        )

    mid = [mid_copy(n, way) for n in range(3) for way in range(2)]
    for n, ref in enumerate(moving):
        mid_out[n] = ref[mine, :]
    start(mid)

    def take(n, way, lo, hi):
        base = OWN + (128 if way else -128)
        moving[n][base + lo : base + hi, :] = mid_in[way, n, lo:hi, :]

    for copy in mid[:2]:
        copy.wait_recv()
    for n in range(5):
        take(n, 0, 64, 128)
        take(n, 1, 0, 64)
    stresses((-3, 11))
    velocities((-2, 10))
    stresses((-1, 9))
    velocities((0, 8))
    stresses((1, 7))
    velocities((2, 6))
    stresses((3, 5))
    for copy in mid[2:]:
        copy.wait_recv()
    for n in range(5):
        take(n, 0, 0 if n < 2 else 16, 64)
        take(n, 1, 64, 128 if n < 2 else 112)
    for lo in (-7, -5, -3, -1):
        stresses((lo, lo + 4), (4 - lo, 8 - lo))
        if lo < -1:
            velocities((lo + 1, lo + 5), (3 - lo, 7 - lo))
    velocities((0, 8))

    turn = jnp.where(odd == 1, (row128 + lane128 == 127).astype(F32), eye.astype(F32)).astype(BF16)
    sign_u = (1 - 2 * odd).astype(F32)
    for i in range(8):
        uo, vo, _, _ = forcing_row(f_all, 8 + i)
        (u,), (v,), (p,) = (rows_of(ref, 9 + i, 1) for ref in (u_all, v_all, p_all))
        du = u - uo
        dv = v - vo
        speed = jnp.where(p > 0.0, jnp.sqrt(du * du + dv * dv), 0.0)
        du = sign_u * (speed * du)
        dv = speed * dv
        both = jnp.concatenate([du[0:8], dv[0:8], du[8:16], dv[8:16]], axis=0).astype(BF16)
        send_d[32 * i : 32 * i + 32, :] = dot(both, turn).astype(BF16)

    def drag_copy(n):
        g = other(n)
        return remote(
            rows_at(send_d, landing(g, odd) * 16, 16),
            rows_at(recv_d, face * 16, 16),
            d_send.at[n],
            d_recv.at[n],
            (g, tile),
        )

    def drag_start(n, carry):
        drag_copy(n).start()
        return carry

    lax.fori_loop(0, 15, drag_start, 0)
    recv_d[pl.ds(pl.multiple_of(face * 16, 16), 16), :] = send_d[
        pl.ds(pl.multiple_of(landing(face, odd) * 16, 16), 16), :
    ]

    def finish(mirrored):
        for b in range(ROW):
            spot = pl.ds(OWN + (ROW - 1 - b if mirrored else b), 8, stride=ROW)
            cols = slice(128 * b, 128 * b + 128)
            u = u_all[spot, :]
            v = v_all[spot, :]
            vel_out[0, :, cols] = -flip_lanes(u) if mirrored else u
            vel_out[1, :, cols] = flip_lanes(v) if mirrored else v

    @pl.when(odd == 0)
    def _():
        finish(False)

    @pl.when(odd == 1)
    def _():
        finish(True)

    def sent(n, carry):
        forcing_copy(n).wait_send()
        return carry

    lax.fori_loop(0, 15, sent, 0)

    for copy in mid + forcing_halo:
        copy.wait_send()

    def returned(n, carry):
        drag_copy(n).wait()
        return carry

    lax.fori_loop(0, 15, returned, 0)
    back = recv_d[...].astype(F32)
    for c in range(2):
        part = jnp.concatenate(
            [back[16 * g + 8 * c : 16 * g + 8 * c + 8] for g in range(16)], axis=0
        ).astype(BF16)
        unsorted[pl.ds(c, 128, stride=2), :] = dot(unsort[...], part)
    drag_out[...] = unsorted[...].astype(BF16)


def per_device(ocean_forcing, ice_owner, ice_mask, ice_velocity, ice_mass, ice_strength):
    field = pltpu.VMEM((26 * ROW, 128), F32)
    dma = pltpu.SemaphoreType.DMA
    velocity, drag = pl.pallas_call(
        kernel,
        out_shape=(pltpu.VMEM((2, 8, 2048), F32), pltpu.VMEM((256, 128), BF16)),
        in_specs=[pl.BlockSpec(memory_space=pl.ANY)] * 6,
        out_specs=[pl.BlockSpec(memory_space=pltpu.VMEM)] * 2,
        scratch_shapes=[
            pltpu.VMEM((512, 128), BF16),
            pltpu.VMEM((1, 128), jnp.int32),
            pltpu.VMEM((1, 128), jnp.int32),
            pltpu.VMEM((2, 8, 2048), F32),
            pltpu.VMEM((8, 2048), F32),
            pltpu.VMEM((8, 2048), F32),
            pltpu.VMEM((1024, 128), F32),
            pltpu.VMEM((512, 128), BF16),
            pltpu.VMEM((3 * 512, 128), BF16),
        ]
        + [field] * 7
        + [
            pltpu.VMEM((5, 128, 128), F32),
            pltpu.VMEM((2, 5, 128, 128), F32),
            pltpu.VMEM((256, 128), BF16),
            pltpu.VMEM((256, 128), BF16),
            pltpu.VMEM((128, 128), BF16),
            pltpu.VMEM((256, 128), F32),
            dma((6,)),
            dma((15,)),
            dma((16,)),
            dma((8,)),
            dma((8,)),
            dma((2,)),
            dma((2,)),
            dma((6,)),
            dma((6,)),
            dma((15,)),
            dma((15,)),
            pltpu.SemaphoreType.REGULAR,
        ],
        compiler_params=pltpu.CompilerParams(
            collective_id=0, has_side_effects=True, vmem_limit_bytes=60 * 2**20
        ),
    )(
        ocean_forcing.reshape(512, 128),
        ice_owner,
        ice_mask,
        ice_velocity.reshape(2, 8, 2048),
        ice_mass.reshape(8, 2048),
        ice_strength.reshape(8, 2048),
    )
    return velocity.reshape(2, 1, 8, 2048), drag.reshape(1, 128, 2, 128)


def solution(mesh):
    in_specs = (
        P("face", "tile", None, None),
        P("face", "tile"),
        P("face", "tile"),
        P(None, "face", "tile", None),
        P("face", "tile", None),
        P("face", "tile", None),
    )
    out_specs = (P(None, "face", "tile", None), P("face", "tile", None, None))
    return jax.shard_map(
        per_device, mesh=mesh, in_specs=in_specs, out_specs=out_specs, check_vma=False
    )
```

```python
import jax
import jax.numpy as jnp
from jax import lax
from jax.experimental import pallas as pl
from jax.experimental.pallas import tpu as pltpu
from jax.sharding import PartitionSpec as P

MESH = pl.DeviceIdType.MESH
F32 = jnp.float32
BF16 = jnp.bfloat16
ROW = 16
OWN = 9 * ROW
F_OWN = 512


def iota(shape, dim):
    return lax.broadcasted_iota(jnp.int32, shape, dim)


def dot(a, b):
    return jnp.dot(a, b, preferred_element_type=F32)


def flip_lanes(x):
    return jnp.take_along_axis(x, 127 - iota(x.shape, 1), axis=1)


def centred_x(x):
    lane = iota(x.shape, 1)
    ahead = pltpu.roll(x, 127, 1)
    behind = pltpu.roll(x, 1, 1)
    ahead = jnp.where(lane == 127, pltpu.roll(ahead, ROW - 1, 0), ahead)
    behind = jnp.where(lane == 0, pltpu.roll(behind, 1, 0), behind)
    return ahead - behind


def rows_of(ref, first, count):
    return [ref[(first + n) * ROW : (first + n + 1) * ROW, :] for n in range(count)]


def put_row(ref, row, value):
    ref[row * ROW : (row + 1) * ROW, :] = value


def stress_rows(first, count, u_ref, v_ref, stress, p_ref):
    us = rows_of(u_ref, first - 1, count + 2)
    vs = rows_of(v_ref, first - 1, count + 2)
    ps = rows_of(p_ref, first, count)
    old = [rows_of(s, first, count) for s in stress]
    third = F32(2.0 / 3.0)
    for n in range(count):
        e11 = centred_x(us[n + 1])
        e22 = vs[n + 2] - vs[n]
        shear = (us[n + 2] - us[n]) + centred_x(vs[n + 1])
        dd = e11 + e22
        dtn = e11 - e22
        inv = lax.rsqrt(dd * dd + 0.25 * (dtn * dtn + shear * shear) + 0.04)
        grip = ps[n] * inv
        put_row(stress[0], first + n, third * old[0][n] + (grip * dd - ps[n]))
        put_row(stress[1], first + n, third * old[1][n] + 0.25 * (grip * dtn))
        put_row(stress[2], first + n, third * old[2][n] + 0.125 * (grip * shear))


def forcing_row(f_ref, row):
    block = f_ref[row * 64 : row * 64 + 64, :].astype(F32)
    return [
        jnp.concatenate([block[8 * c : 8 * c + 8], block[32 + 8 * c : 40 + 8 * c]], axis=0)
        for c in range(4)
    ]


def momentum_rows(first, count, cor, u_ref, v_ref, stress, p_ref, m_ref, f_ref):
    s1 = rows_of(stress[0], first - 1, count + 2)
    s2 = rows_of(stress[1], first - 1, count + 2)
    s12 = rows_of(stress[2], first - 1, count + 2)
    us = rows_of(u_ref, first, count)
    vs = rows_of(v_ref, first, count)
    ps = rows_of(p_ref, first, count)
    ms = rows_of(m_ref, first, count)
    for n in range(count):
        uo, vo, tx, ty = forcing_row(f_ref, first + n - 1)
        u, v, m = us[n], vs[n], ms[n]
        fx = 0.25 * centred_x(s1[n + 1] + s2[n + 1]) + 0.5 * (s12[n + 2] - s12[n])
        fy = 0.5 * centred_x(s12[n + 1]) + 0.25 * ((s1[n + 2] - s2[n + 2]) - (s1[n] - s2[n]))
        du = uo - u
        dv = vo - v
        speed = jnp.sqrt(du * du + dv * dv)
        row = first + n
        sign = cor[0] if row < 9 else cor[1] if row < 17 else cor[2]
        turn = sign * m
        inv = jnp.where(ps[n] > 0.0, 1.0 / (m + 0.25 * speed), 0.0)
        put_row(u_ref, first + n, (m * u + 0.25 * (fx + tx + speed * uo + turn * v)) * inv)
        put_row(v_ref, first + n, (m * v + 0.25 * (fy + ty + speed * vo - turn * u)) * inv)


def kernel(
    forcing_hbm, owner_hbm, mask_hbm, vel_hbm, mass_hbm, strength_hbm,
    vel_out, drag_out,
    x_in, owner_in, mask_in, vel_in, mass_in, strength_in,
    spread, send_f, f_all, u_all, v_all, p_all, m_all, a1, a2, a12,
    mid_out, mid_in, send_d, recv_d, unsort,
    in_sem, f_send, f_recv, h_send, h_recv, g_send, g_recv,
    k_send, k_recv, d_send, d_recv, edge,
):
    face = lax.axis_index("face")
    tile = lax.axis_index("tile")
    faces = lax.axis_size("face")
    tiles = lax.axis_size("tile")
    ring = face * tiles + tile

    def along(step):
        there = lax.rem(ring + step + faces * tiles, faces * tiles)
        return lax.div(there, tiles), lax.rem(there, tiles)

    above, below = along(1), along(-1)
    chip = lax.div(face, 2)
    first = tile == 0
    last = tile == tiles - 1
    odd = lax.rem(chip, 2)
    swap = 1 - 2 * lax.rem(face, 2)

    def other(n):
        half = lax.div(n + 1, 2)
        return lax.rem(face + 8 + jnp.where(lax.rem(n, 2) == 0, half, -half), faces)

    def remote(src, dst, send_sem, recv_sem, there):
        return pltpu.make_async_remote_copy(
            src_ref=src,
            dst_ref=dst,
            send_sem=send_sem,
            recv_sem=recv_sem,
            device_id=there,
            device_id_type=MESH,
        )

    def rows_at(ref, start, size):
        return ref.at[pl.ds(pl.multiple_of(start, 16), size), :]

    loads = [
        pltpu.make_async_copy(src, dst, in_sem.at[n])
        for n, (src, dst) in enumerate(
            [
                (vel_hbm, vel_in),
                (strength_hbm, strength_in),
                (mass_hbm, mass_in),
                (mask_hbm, mask_in),
                (owner_hbm, owner_in),
                (forcing_hbm, x_in),
            ]
        )
    ]
    for load in loads:
        load.start()

    barrier = pltpu.get_barrier_semaphore()

    def greet(there):
        pl.semaphore_signal(barrier, inc=1, device_id=there, device_id_type=MESH)

    def greet_face(n, carry):
        greet((other(n), tile))
        return carry

    greet(below)

    @pl.when(jnp.logical_not(last))
    def _():
        greet(above)

    lax.fori_loop(0, 15, greet_face, 0)
    row128 = iota((128, 128), 0)
    lane128 = iota((128, 128), 1)
    eye = row128 == lane128
    ones = jnp.ones((128, 128), BF16)
    mirror = (row128 + lane128 == 127).astype(F32).astype(BF16)
    for load in loads[:4]:
        load.wait()
    mask_lanes = jnp.broadcast_to(mask_in[...].astype(F32), (128, 128))
    flipped = row128 ^ (odd * 15)
    cover = dot(jnp.where(flipped == lane128, mask_lanes, 0.0).astype(BF16), ones)

    def stage(mirrored):
        for b in range(ROW):
            spot = pl.ds(OWN + (ROW - 1 - b if mirrored else b), 8, stride=ROW)
            cols = slice(128 * b, 128 * b + 128)
            turned = flip_lanes if mirrored else (lambda value: value)
            u = turned(vel_in[0, :, cols])
            u_all[spot, :] = -u if mirrored else u
            v_all[spot, :] = turned(vel_in[1, :, cols])
            p_all[spot, :] = turned(strength_in[:, cols])
            m_all[spot, :] = turned(mass_in[:, cols])

    @pl.when(odd == 0)
    def _():
        stage(False)

    @pl.when(odd == 1)
    def _():
        stage(True)

    mine = slice(OWN, OWN + 128)
    p_all[mine, :] = p_all[mine, :] * cover * F32(1.0 / 3.0)

    state = (u_all, v_all, p_all, m_all)

    def state_copies(shift, way, there, send_sem, recv_sem):
        lo = (0, 0, 0, 0) if way else (0, 0, 16, 32)
        hi = (128, 128, 112, 96) if way else (128, 128, 128, 128)
        return [
            remote(
                ref.at[OWN + lo[n] : OWN + hi[n], :],
                ref.at[OWN + shift + lo[n] : OWN + shift + hi[n], :],
                send_sem.at[2 * n + way],
                recv_sem.at[2 * n + way],
                there,
            )
            for n, ref in enumerate(state)
        ]

    near_up = state_copies(-128, 0, above, h_send, h_recv)
    near_down = state_copies(128, 1, below, h_send, h_recv)

    def start(copies):
        for copy in copies:
            copy.start()

    def landing(f, odd_there):
        return f + odd_there * (1 - 2 * lax.rem(f, 2))

    pl.semaphore_wait(barrier, 16 + jnp.minimum(tile, 1))

    @pl.when(last)
    def _():
        pl.semaphore_signal(edge, inc=1, device_id=above, device_id_type=MESH)

    start(near_up)

    @pl.when(jnp.logical_not(first))
    def _():
        start(near_down)


    loads[4].wait()
    owner = owner_in[...]
    owner_lanes = jnp.broadcast_to(owner, (128, 128))
    owner_rows = dot(jnp.where(eye, owner_lanes.astype(F32), 0.0).astype(BF16), ones)
    same = (owner_rows == owner_lanes.astype(F32)) & (row128 <= lane128)
    rank = jnp.sum(same.astype(F32), axis=0, keepdims=True) - 1.0
    owner_odd = (owner & 2) == 2
    rank = jnp.where(owner_odd, 7.0 - rank, rank)
    place = owner.astype(F32) * 8.0 + rank
    place_lanes = jnp.broadcast_to(place, (128, 128))
    sorter = jnp.where(row128.astype(F32) == place_lanes, 1.0, 0.0)
    slot_odd = (row128 & 16) == 16
    sorter = jnp.concatenate(
        [jnp.where(slot_odd, 0.0, sorter), jnp.where(slot_odd, sorter, 0.0)], axis=1
    ).astype(BF16)
    loads[5].wait()
    x = x_in[...]
    spread[0:512, :] = x.astype(F32)
    sign_x = jnp.where((iota((512, 128), 0) & 1) == 0, -1.0, 1.0)
    spread[512:1024, :] = dot(x, mirror) * sign_x
    wide = jnp.concatenate(
        [
            jnp.concatenate(
                [spread[pl.ds(512 * n + c, 128, stride=4), :].astype(BF16) for c in range(4)],
                axis=1,
            )
            for n in range(2)
        ],
        axis=0,
    )
    grouped = dot(sorter, wide)
    for g in range(16):
        send_f[32 * g : 32 * g + 32, :] = jnp.concatenate(
            [grouped[8 * g : 8 * g + 8, 128 * c : 128 * c + 128] for c in range(4)], axis=0
        ).astype(BF16)

    def forcing_copy(n):
        g = other(n)
        there = landing(face, lax.rem(lax.div(g, 2), 2))
        return remote(
            rows_at(send_f, g * 32, 32),
            rows_at(f_all, F_OWN + there * 32, 32),
            f_send.at[n],
            f_recv.at[face],
            (g, tile),
        )

    def forcing_start(n, carry):
        forcing_copy(n).start()
        return carry

    lax.fori_loop(0, 15, forcing_start, 0)

    f_all[pl.ds(pl.multiple_of(F_OWN + landing(face, odd) * 32, 32), 32), :] = send_f[
        pl.ds(pl.multiple_of(face * 32, 32), 32), :
    ]

    row256 = iota((256, 128), 0)
    lane256 = iota((256, 128), 1)
    picked = jnp.where(row256 // 2 == lane256, jnp.broadcast_to(place, (256, 128)), 0.0)
    place_rows = dot(picked.astype(BF16), ones)
    slot = (lane256 // 16) * 8 + lane256 % 8
    slot = jnp.where(row256 % 2 == lane256 // 8 % 2, slot, -128).astype(F32)
    unsort[:, 0:128] = jnp.where(place_rows == slot, 1.0, 0.0).astype(BF16)
    unsort[:, 128:256] = jnp.where(place_rows - 64.0 == slot, 1.0, 0.0).astype(BF16)
    for ref in (a1, a2, a12):
        ref[...] = jnp.zeros_like(ref)

    def forcing_row_copy(start, size, way):
        shift = 512 if way else -512
        return remote(
            rows_at(f_all, F_OWN + start, size),
            rows_at(f_all, F_OWN + shift + start, size),
            g_send.at[way],
            g_recv.at[way],
            below if way else above,
        )

    def arrived(f):
        place = landing(f, odd)
        remote(
            rows_at(send_f, 0, 32),
            rows_at(f_all, F_OWN + place * 32, 32),
            f_send.at[0],
            f_recv.at[f],
            above,
        ).wait_recv()

    def pass_row(n, carry):
        step = jnp.where(lax.rem(n, 2) == 1, lax.div(n + 1, 2), 8 - lax.div(n, 2))
        row = lax.rem(chip + step, 8)

        @pl.when(n == 0)
        def _():
            arrived(face + swap)

        @pl.when(n > 0)
        def _():
            arrived(2 * row)
            arrived(2 * row + 1)

        @pl.when(row >= 2)
        def _():
            forcing_row_copy(row * 64, 64, 0).start()

        @pl.when((row < 6) & jnp.logical_not(first))
        def _():
            forcing_row_copy(row * 64, 64, 1).start()

        return carry

    lax.fori_loop(0, 8, pass_row, 0)

    @pl.when(first)
    def _():
        pl.semaphore_wait(edge, 1)
        start(near_down)
        forcing_row_copy(0, 384, 1).start()

    cor = [
        0.5 - lax.rem(lax.div(f, 2), 2).astype(F32) for f in (below[0], face, above[0])
    ]
    stress = (a1, a2, a12)

    def stresses(*parts):
        for lo, hi in parts:
            stress_rows(9 + lo, hi - lo, u_all, v_all, stress, p_all)

    def velocities(*parts):
        for lo, hi in parts:
            momentum_rows(9 + lo, hi - lo, cor, u_all, v_all, stress, p_all, m_all, f_all)

    for copy in near_up + near_down:
        copy.wait_recv()
    stresses((-7, 15))
    for copy in near_up + near_down:
        copy.wait_send()
    velocities((0, 8))
    stresses((1, 7))
    velocities((2, 6))
    stresses((3, 5))
    forcing_halo = [forcing_row_copy(128, 384, 0), forcing_row_copy(0, 384, 1)]
    for copy in forcing_halo:
        copy.wait_recv()
    velocities((-6, 0), (8, 14))
    stresses((-5, 1), (7, 13))
    velocities((-4, 2), (6, 12))
    stresses((-3, 3), (5, 11))
    velocities((-2, 10))
    stresses((-1, 9))
    velocities((0, 8))

    moving = (u_all, v_all, a1, a2, a12)

    def mid_copy(n, way):
        lo, hi = [((64, 128), (0, 64), (16, 64)), ((0, 64), (64, 128), (64, 112))][way][n]
        fields = (slice(0, 5), slice(0, 2), slice(2, 5))[n]
        return remote(
            mid_out.at[fields, lo:hi, :],
            mid_in.at[way, fields, lo:hi, :],
            k_send.at[2 * n + way],
            k_recv.at[2 * n + way],
            below if way else above,
        )

    mid = [mid_copy(n, way) for n in range(3) for way in range(2)]
    for n, ref in enumerate(moving):
        mid_out[n] = ref[mine, :]
    start(mid)

    def take(n, way, lo, hi):
        base = OWN + (128 if way else -128)
        moving[n][base + lo : base + hi, :] = mid_in[way, n, lo:hi, :]

    for copy in mid[:2]:
        copy.wait_recv()
    for n in range(5):
        take(n, 0, 64, 128)
        take(n, 1, 0, 64)
    stresses((-3, 11))
    velocities((-2, 10))
    stresses((-1, 9))
    velocities((0, 8))
    stresses((1, 7))
    velocities((2, 6))
    stresses((3, 5))
    for copy in mid[2:]:
        copy.wait_recv()
    for n in range(5):
        take(n, 0, 0 if n < 2 else 16, 64)
        take(n, 1, 64, 128 if n < 2 else 112)
    for lo in (-7, -5, -3, -1):
        stresses((lo, lo + 4), (4 - lo, 8 - lo))
        if lo < -1:
            velocities((lo + 1, lo + 5), (3 - lo, 7 - lo))
    velocities((0, 8))

    turn = jnp.where(odd == 1, (row128 + lane128 == 127).astype(F32), eye.astype(F32)).astype(BF16)
    sign_u = (1 - 2 * odd).astype(F32)
    for i in range(8):
        uo, vo, _, _ = forcing_row(f_all, 8 + i)
        (u,), (v,), (p,) = (rows_of(ref, 9 + i, 1) for ref in (u_all, v_all, p_all))
        du = u - uo
        dv = v - vo
        speed = jnp.where(p > 0.0, jnp.sqrt(du * du + dv * dv), 0.0)
        du = sign_u * (speed * du)
        dv = speed * dv
        both = jnp.concatenate([du[0:8], dv[0:8], du[8:16], dv[8:16]], axis=0).astype(BF16)
        send_d[32 * i : 32 * i + 32, :] = dot(both, turn).astype(BF16)

    def drag_copy(n):
        g = other(n)
        return remote(
            rows_at(send_d, landing(g, odd) * 16, 16),
            rows_at(recv_d, face * 16, 16),
            d_send.at[n],
            d_recv.at[n],
            (g, tile),
        )

    drag_copies = [drag_copy(n) for n in range(15)]
    start(drag_copies)
    recv_d[pl.ds(pl.multiple_of(face * 16, 16), 16), :] = send_d[
        pl.ds(pl.multiple_of(landing(face, odd) * 16, 16), 16), :
    ]

    def finish(mirrored):
        for b in range(ROW):
            spot = pl.ds(OWN + (ROW - 1 - b if mirrored else b), 8, stride=ROW)
            cols = slice(128 * b, 128 * b + 128)
            u = u_all[spot, :]
            v = v_all[spot, :]
            vel_out[0, :, cols] = -flip_lanes(u) if mirrored else u
            vel_out[1, :, cols] = flip_lanes(v) if mirrored else v

    @pl.when(odd == 0)
    def _():
        finish(False)

    @pl.when(odd == 1)
    def _():
        finish(True)

    def sent(n, carry):
        forcing_copy(n).wait_send()
        return carry

    lax.fori_loop(0, 15, sent, 0)

    for copy in mid + forcing_halo:
        copy.wait_send()

    for copy in drag_copies:
        copy.wait_recv()
    drag_out[...] = dot(unsort[...], recv_d[...]).astype(BF16)
    for copy in drag_copies:
        copy.wait_send()


def per_device(ocean_forcing, ice_owner, ice_mask, ice_velocity, ice_mass, ice_strength):
    field = pltpu.VMEM((26 * ROW, 128), F32)
    dma = pltpu.SemaphoreType.DMA
    velocity, drag = pl.pallas_call(
        kernel,
        out_shape=(pltpu.VMEM((2, 8, 2048), F32), pltpu.VMEM((256, 128), BF16)),
        in_specs=[pl.BlockSpec(memory_space=pl.ANY)] * 6,
        out_specs=[pl.BlockSpec(memory_space=pltpu.VMEM)] * 2,
        scratch_shapes=[
            pltpu.VMEM((512, 128), BF16),
            pltpu.VMEM((1, 128), jnp.int32),
            pltpu.VMEM((1, 128), jnp.int32),
            pltpu.VMEM((2, 8, 2048), F32),
            pltpu.VMEM((8, 2048), F32),
            pltpu.VMEM((8, 2048), F32),
            pltpu.VMEM((1024, 128), F32),
            pltpu.VMEM((512, 128), BF16),
            pltpu.VMEM((3 * 512, 128), BF16),
        ]
        + [field] * 7
        + [
            pltpu.VMEM((5, 128, 128), F32),
            pltpu.VMEM((2, 5, 128, 128), F32),
            pltpu.VMEM((256, 128), BF16),
            pltpu.VMEM((256, 128), BF16),
            pltpu.VMEM((256, 256), BF16),
            dma((6,)),
            dma((15,)),
            dma((16,)),
            dma((8,)),
            dma((8,)),
            dma((2,)),
            dma((2,)),
            dma((6,)),
            dma((6,)),
            dma((15,)),
            dma((15,)),
            pltpu.SemaphoreType.REGULAR,
        ],
        compiler_params=pltpu.CompilerParams(
            collective_id=0, has_side_effects=True, vmem_limit_bytes=60 * 2**20
        ),
    )(
        ocean_forcing.reshape(512, 128),
        ice_owner,
        ice_mask,
        ice_velocity.reshape(2, 8, 2048),
        ice_mass.reshape(8, 2048),
        ice_strength.reshape(8, 2048),
    )
    return velocity.reshape(2, 1, 8, 2048), drag.reshape(1, 128, 2, 128)


def solution(mesh):
    in_specs = (
        P("face", "tile", None, None),
        P("face", "tile"),
        P("face", "tile"),
        P(None, "face", "tile", None),
        P("face", "tile", None),
        P("face", "tile", None),
    )
    out_specs = (P(None, "face", "tile", None), P("face", "tile", None, None))
    return jax.shard_map(
        per_device, mesh=mesh, in_specs=in_specs, out_specs=out_specs, check_vma=False
    )
```

```python
import jax
import jax.numpy as jnp
from jax import lax
from jax.experimental import pallas as pl
from jax.experimental.pallas import tpu as pltpu
from jax.sharding import PartitionSpec as P

MESH = pl.DeviceIdType.MESH
F32 = jnp.float32
BF16 = jnp.bfloat16
ROW = 16
OWN = 9 * ROW
F_OWN = 512


def iota(shape, dim):
    return lax.broadcasted_iota(jnp.int32, shape, dim)


def dot(a, b):
    return jnp.dot(a, b, preferred_element_type=F32)


def flip_lanes(x):
    return jnp.take_along_axis(x, 127 - iota(x.shape, 1), axis=1)


def centred_x(x):
    lane = iota(x.shape, 1)
    ahead = pltpu.roll(x, 127, 1)
    behind = pltpu.roll(x, 1, 1)
    ahead = jnp.where(lane == 127, pltpu.roll(ahead, ROW - 1, 0), ahead)
    behind = jnp.where(lane == 0, pltpu.roll(behind, 1, 0), behind)
    return ahead - behind


def rows_of(ref, first, count):
    return [ref[(first + n) * ROW : (first + n + 1) * ROW, :] for n in range(count)]


def put_row(ref, row, value):
    ref[row * ROW : (row + 1) * ROW, :] = value


def stress_rows(first, count, u_ref, v_ref, stress, p_ref):
    us = rows_of(u_ref, first - 1, count + 2)
    vs = rows_of(v_ref, first - 1, count + 2)
    ps = rows_of(p_ref, first, count)
    old = [rows_of(s, first, count) for s in stress]
    third = F32(2.0 / 3.0)
    for n in range(count):
        e11 = centred_x(us[n + 1])
        e22 = vs[n + 2] - vs[n]
        shear = (us[n + 2] - us[n]) + centred_x(vs[n + 1])
        dd = e11 + e22
        dtn = e11 - e22
        inv = lax.rsqrt(dd * dd + 0.25 * (dtn * dtn + shear * shear) + 0.04)
        grip = ps[n] * inv
        put_row(stress[0], first + n, third * old[0][n] + (grip * dd - ps[n]))
        put_row(stress[1], first + n, third * old[1][n] + 0.25 * (grip * dtn))
        put_row(stress[2], first + n, third * old[2][n] + 0.125 * (grip * shear))


def forcing_row(f_ref, row):
    block = f_ref[row * 64 : row * 64 + 64, :].astype(F32)
    return [
        jnp.concatenate([block[8 * c : 8 * c + 8], block[32 + 8 * c : 40 + 8 * c]], axis=0)
        for c in range(4)
    ]


def momentum_rows(first, count, cor, u_ref, v_ref, stress, p_ref, m_ref, f_ref):
    s1 = rows_of(stress[0], first - 1, count + 2)
    s2 = rows_of(stress[1], first - 1, count + 2)
    s12 = rows_of(stress[2], first - 1, count + 2)
    us = rows_of(u_ref, first, count)
    vs = rows_of(v_ref, first, count)
    ps = rows_of(p_ref, first, count)
    ms = rows_of(m_ref, first, count)
    for n in range(count):
        uo, vo, tx, ty = forcing_row(f_ref, first + n - 1)
        u, v, m = us[n], vs[n], ms[n]
        fx = 0.25 * centred_x(s1[n + 1] + s2[n + 1]) + 0.5 * (s12[n + 2] - s12[n])
        fy = 0.5 * centred_x(s12[n + 1]) + 0.25 * ((s1[n + 2] - s2[n + 2]) - (s1[n] - s2[n]))
        du = uo - u
        dv = vo - v
        speed = jnp.sqrt(du * du + dv * dv)
        row = first + n
        sign = cor[0] if row < 9 else cor[1] if row < 17 else cor[2]
        turn = sign * m
        inv = jnp.where(ps[n] > 0.0, 1.0 / (m + 0.25 * speed), 0.0)
        put_row(u_ref, first + n, (m * u + 0.25 * (fx + tx + speed * uo + turn * v)) * inv)
        put_row(v_ref, first + n, (m * v + 0.25 * (fy + ty + speed * vo - turn * u)) * inv)


def kernel(
    forcing_hbm, owner_hbm, mask_hbm, vel_hbm, mass_hbm, strength_hbm,
    vel_out, drag_out,
    x_in, owner_in, mask_in, vel_in, mass_in, strength_in,
    spread, send_f, f_all, u_all, v_all, p_all, m_all, a1, a2, a12,
    mid_out, mid_in, send_d, recv_d, unsort, unsorted,
    in_sem, f_send, f_recv, h_send, h_recv, g_send, g_recv,
    k_send, k_recv, d_send, d_recv, edge,
):
    face = lax.axis_index("face")
    tile = lax.axis_index("tile")
    faces = lax.axis_size("face")
    tiles = lax.axis_size("tile")
    ring = face * tiles + tile

    def along(step):
        there = lax.rem(ring + step + faces * tiles, faces * tiles)
        return lax.div(there, tiles), lax.rem(there, tiles)

    above, below = along(1), along(-1)
    chip = lax.div(face, 2)
    first = tile == 0
    last = tile == tiles - 1
    odd = lax.rem(chip, 2)
    swap = 1 - 2 * lax.rem(face, 2)

    def other(n):
        half = lax.div(n + 1, 2)
        return lax.rem(face + 8 + jnp.where(lax.rem(n, 2) == 0, half, -half), faces)

    def remote(src, dst, send_sem, recv_sem, there):
        return pltpu.make_async_remote_copy(
            src_ref=src,
            dst_ref=dst,
            send_sem=send_sem,
            recv_sem=recv_sem,
            device_id=there,
            device_id_type=MESH,
        )

    def rows_at(ref, start, size):
        return ref.at[pl.ds(pl.multiple_of(start, 16), size), :]

    loads = [
        pltpu.make_async_copy(src, dst, in_sem.at[n])
        for n, (src, dst) in enumerate(
            [
                (owner_hbm, owner_in),
                (forcing_hbm, x_in),
                (mask_hbm, mask_in),
                (vel_hbm, vel_in),
                (strength_hbm, strength_in),
                (mass_hbm, mass_in),
            ]
        )
    ]
    for load in loads:
        load.start()

    barrier = pltpu.get_barrier_semaphore()

    def greet(there):
        pl.semaphore_signal(barrier, inc=1, device_id=there, device_id_type=MESH)

    def greet_face(n, carry):
        greet((other(n), tile))
        return carry

    lax.fori_loop(0, 15, greet_face, 0)
    greet(below)

    @pl.when(jnp.logical_not(last))
    def _():
        greet(above)

    row128 = iota((128, 128), 0)
    lane128 = iota((128, 128), 1)
    eye = row128 == lane128
    ones = jnp.ones((128, 128), BF16)
    mirror = (row128 + lane128 == 127).astype(F32).astype(BF16)
    loads[0].wait()
    owner = owner_in[...]
    owner_lanes = jnp.broadcast_to(owner, (128, 128))
    owner_rows = dot(jnp.where(eye, owner_lanes.astype(F32), 0.0).astype(BF16), ones)
    same = (owner_rows == owner_lanes.astype(F32)) & (row128 <= lane128)
    rank = jnp.sum(same.astype(F32), axis=0, keepdims=True) - 1.0
    owner_odd = (owner & 2) == 2
    rank = jnp.where(owner_odd, 7.0 - rank, rank)
    place = owner.astype(F32) * 8.0 + rank
    place_lanes = jnp.broadcast_to(place, (128, 128))
    sorter = jnp.where(row128.astype(F32) == place_lanes, 1.0, 0.0)
    slot_odd = (row128 & 16) == 16
    sorter = jnp.concatenate(
        [jnp.where(slot_odd, 0.0, sorter), jnp.where(slot_odd, sorter, 0.0)], axis=1
    ).astype(BF16)
    loads[1].wait()
    x = x_in[...]
    spread[0:512, :] = x.astype(F32)
    sign_x = jnp.where((iota((512, 128), 0) & 1) == 0, -1.0, 1.0)
    spread[512:1024, :] = dot(x, mirror) * sign_x
    wide = jnp.concatenate(
        [
            jnp.concatenate(
                [spread[pl.ds(512 * n + c, 128, stride=4), :].astype(BF16) for c in range(4)],
                axis=1,
            )
            for n in range(2)
        ],
        axis=0,
    )
    grouped = dot(sorter, wide)
    for g in range(16):
        send_f[32 * g : 32 * g + 32, :] = jnp.concatenate(
            [grouped[8 * g : 8 * g + 8, 128 * c : 128 * c + 128] for c in range(4)], axis=0
        ).astype(BF16)

    loads[2].wait()
    mask_lanes = jnp.broadcast_to(mask_in[...].astype(F32), (128, 128))
    flipped = row128 ^ (odd * 15)
    cover = dot(jnp.where(flipped == lane128, mask_lanes, 0.0).astype(BF16), ones)
    for load in loads[3:]:
        load.wait()

    def stage(mirrored):
        for b in range(ROW):
            spot = pl.ds(OWN + (ROW - 1 - b if mirrored else b), 8, stride=ROW)
            cols = slice(128 * b, 128 * b + 128)
            turned = flip_lanes if mirrored else (lambda value: value)
            u = turned(vel_in[0, :, cols])
            u_all[spot, :] = -u if mirrored else u
            v_all[spot, :] = turned(vel_in[1, :, cols])
            p_all[spot, :] = turned(strength_in[:, cols])
            m_all[spot, :] = turned(mass_in[:, cols])

    @pl.when(odd == 0)
    def _():
        stage(False)

    @pl.when(odd == 1)
    def _():
        stage(True)

    mine = slice(OWN, OWN + 128)
    p_all[mine, :] = p_all[mine, :] * cover * F32(1.0 / 3.0)

    state = (u_all, v_all, p_all, m_all)

    def state_copies(shift, way, there, send_sem, recv_sem):
        lo = (0, 0, 0, 0) if way else (0, 0, 16, 32)
        hi = (128, 128, 112, 96) if way else (128, 128, 128, 128)
        return [
            remote(
                ref.at[OWN + lo[n] : OWN + hi[n], :],
                ref.at[OWN + shift + lo[n] : OWN + shift + hi[n], :],
                send_sem.at[2 * n + way],
                recv_sem.at[2 * n + way],
                there,
            )
            for n, ref in enumerate(state)
        ]

    near_up = state_copies(-128, 0, above, h_send, h_recv)
    near_down = state_copies(128, 1, below, h_send, h_recv)

    def start(copies):
        for copy in copies:
            copy.start()

    def landing(f, odd_there):
        return f + odd_there * (1 - 2 * lax.rem(f, 2))

    pl.semaphore_wait(barrier, 16 + jnp.minimum(tile, 1))

    @pl.when(last)
    def _():
        pl.semaphore_signal(edge, inc=1, device_id=above, device_id_type=MESH)

    start(near_up)

    @pl.when(jnp.logical_not(first))
    def _():
        start(near_down)


    def forcing_copy(n):
        g = other(n)
        there = landing(face, lax.rem(lax.div(g, 2), 2))
        return remote(
            rows_at(send_f, g * 32, 32),
            rows_at(f_all, F_OWN + there * 32, 32),
            f_send.at[n],
            f_recv.at[face],
            (g, tile),
        )

    def forcing_start(n, carry):
        forcing_copy(n).start()
        return carry

    lax.fori_loop(0, 15, forcing_start, 0)

    f_all[pl.ds(pl.multiple_of(F_OWN + landing(face, odd) * 32, 32), 32), :] = send_f[
        pl.ds(pl.multiple_of(face * 32, 32), 32), :
    ]

    place_rows = dot(jnp.where(eye, place_lanes, 0.0).astype(BF16), ones)
    unsort[...] = jnp.where(place_rows == lane128.astype(F32), 1.0, 0.0).astype(BF16)
    for ref in (a1, a2, a12):
        ref[...] = jnp.zeros_like(ref)

    def forcing_row_copy(start, size, way):
        shift = 512 if way else -512
        return remote(
            rows_at(f_all, F_OWN + start, size),
            rows_at(f_all, F_OWN + shift + start, size),
            g_send.at[way],
            g_recv.at[way],
            below if way else above,
        )

    def arrived(f):
        place = landing(f, odd)
        remote(
            rows_at(send_f, 0, 32),
            rows_at(f_all, F_OWN + place * 32, 32),
            f_send.at[0],
            f_recv.at[f],
            above,
        ).wait_recv()

    def pass_row(n, carry):
        step = jnp.where(lax.rem(n, 2) == 1, lax.div(n + 1, 2), 8 - lax.div(n, 2))
        row = lax.rem(chip + step, 8)

        @pl.when(n == 0)
        def _():
            arrived(face + swap)

        @pl.when(n > 0)
        def _():
            arrived(2 * row)
            arrived(2 * row + 1)

        @pl.when(row >= 2)
        def _():
            forcing_row_copy(row * 64, 64, 0).start()

        @pl.when((row < 6) & jnp.logical_not(first))
        def _():
            forcing_row_copy(row * 64, 64, 1).start()

        return carry

    lax.fori_loop(0, 8, pass_row, 0)

    @pl.when(first)
    def _():
        pl.semaphore_wait(edge, 1)
        start(near_down)
        forcing_row_copy(0, 384, 1).start()

    cor = [
        0.5 - lax.rem(lax.div(f, 2), 2).astype(F32) for f in (below[0], face, above[0])
    ]
    stress = (a1, a2, a12)

    def stresses(*parts):
        for lo, hi in parts:
            stress_rows(9 + lo, hi - lo, u_all, v_all, stress, p_all)

    def velocities(*parts):
        for lo, hi in parts:
            momentum_rows(9 + lo, hi - lo, cor, u_all, v_all, stress, p_all, m_all, f_all)

    for copy in near_up + near_down:
        copy.wait_recv()
    stresses((-7, 15))
    for copy in near_up + near_down:
        copy.wait_send()
    velocities((0, 8))
    stresses((1, 7))
    velocities((2, 6))
    stresses((3, 5))
    forcing_halo = [forcing_row_copy(128, 384, 0), forcing_row_copy(0, 384, 1)]
    for copy in forcing_halo:
        copy.wait_recv()
    velocities((-6, 0), (8, 14))
    stresses((-5, 1), (7, 13))
    velocities((-4, 2), (6, 12))
    stresses((-3, 3), (5, 11))
    velocities((-2, 10))
    stresses((-1, 9))

    moving = (u_all, v_all, a1, a2, a12)

    def mid_copy(n, way):
        lo, hi = [
            ((64, 128), (64, 128), (16, 64), (0, 64)),
            ((0, 64), (0, 64), (64, 112), (64, 128)),
        ][way][n]
        fields = slice(0, 2) if n % 2 else slice(2, 5)
        return remote(
            mid_out.at[fields, lo:hi, :],
            mid_in.at[way, fields, lo:hi, :],
            k_send.at[2 * n + way],
            k_recv.at[2 * n + way],
            below if way else above,
        )

    mid = [mid_copy(n, way) for n in range(4) for way in range(2)]
    for n in range(2, 5):
        mid_out[n] = moving[n][mine, :]
    start(mid[:2])
    velocities((0, 8))
    for n in range(2):
        mid_out[n] = moving[n][mine, :]
    start(mid[2:])

    def take(n, way, lo, hi):
        base = OWN + (128 if way else -128)
        moving[n][base + lo : base + hi, :] = mid_in[way, n, lo:hi, :]

    for copy in mid[:4]:
        copy.wait_recv()
    for n in range(5):
        take(n, 0, 64, 128)
        take(n, 1, 0, 64)
    stresses((-3, 11))
    velocities((-2, 10))
    stresses((-1, 9))
    velocities((0, 8))
    stresses((1, 7))
    velocities((2, 6))
    stresses((3, 5))
    for copy in mid[4:]:
        copy.wait_recv()
    for n in range(5):
        take(n, 0, 0 if n < 2 else 16, 64)
        take(n, 1, 64, 128 if n < 2 else 112)
    for lo in (-7, -5, -3, -1):
        stresses((lo, lo + 4), (4 - lo, 8 - lo))
        if lo < -1:
            velocities((lo + 1, lo + 5), (3 - lo, 7 - lo))
    velocities((0, 8))

    turn = jnp.where(odd == 1, (row128 + lane128 == 127).astype(F32), eye.astype(F32)).astype(BF16)
    sign_u = (1 - 2 * odd).astype(F32)
    for i in range(8):
        uo, vo, _, _ = forcing_row(f_all, 8 + i)
        (u,), (v,), (p,) = (rows_of(ref, 9 + i, 1) for ref in (u_all, v_all, p_all))
        du = u - uo
        dv = v - vo
        speed = jnp.where(p > 0.0, jnp.sqrt(du * du + dv * dv), 0.0)
        du = sign_u * (speed * du)
        dv = speed * dv
        both = jnp.concatenate([du[0:8], dv[0:8], du[8:16], dv[8:16]], axis=0).astype(BF16)
        send_d[32 * i : 32 * i + 32, :] = dot(both, turn).astype(BF16)

    def drag_copy(n):
        g = other(n)
        return remote(
            rows_at(send_d, landing(g, odd) * 16, 16),
            rows_at(recv_d, face * 16, 16),
            d_send.at[n],
            d_recv.at[n],
            (g, tile),
        )

    def drag_start(n, carry):
        drag_copy(n).start()
        return carry

    lax.fori_loop(0, 15, drag_start, 0)
    recv_d[pl.ds(pl.multiple_of(face * 16, 16), 16), :] = send_d[
        pl.ds(pl.multiple_of(landing(face, odd) * 16, 16), 16), :
    ]

    def finish(mirrored):
        for b in range(ROW):
            spot = pl.ds(OWN + (ROW - 1 - b if mirrored else b), 8, stride=ROW)
            cols = slice(128 * b, 128 * b + 128)
            u = u_all[spot, :]
            v = v_all[spot, :]
            vel_out[0, :, cols] = -flip_lanes(u) if mirrored else u
            vel_out[1, :, cols] = flip_lanes(v) if mirrored else v

    @pl.when(odd == 0)
    def _():
        finish(False)

    @pl.when(odd == 1)
    def _():
        finish(True)

    def sent(n, carry):
        forcing_copy(n).wait_send()
        return carry

    lax.fori_loop(0, 15, sent, 0)

    for copy in mid + forcing_halo:
        copy.wait_send()

    def returned(n, carry):
        drag_copy(n).wait()
        return carry

    lax.fori_loop(0, 15, returned, 0)
    back = recv_d[...].astype(F32)
    for c in range(2):
        part = jnp.concatenate(
            [back[16 * g + 8 * c : 16 * g + 8 * c + 8] for g in range(16)], axis=0
        ).astype(BF16)
        unsorted[pl.ds(c, 128, stride=2), :] = dot(unsort[...], part)
    drag_out[...] = unsorted[...].astype(BF16)


def per_device(ocean_forcing, ice_owner, ice_mask, ice_velocity, ice_mass, ice_strength):
    field = pltpu.VMEM((26 * ROW, 128), F32)
    dma = pltpu.SemaphoreType.DMA
    velocity, drag = pl.pallas_call(
        kernel,
        out_shape=(pltpu.VMEM((2, 8, 2048), F32), pltpu.VMEM((256, 128), BF16)),
        in_specs=[pl.BlockSpec(memory_space=pl.ANY)] * 6,
        out_specs=[pl.BlockSpec(memory_space=pltpu.VMEM)] * 2,
        scratch_shapes=[
            pltpu.VMEM((512, 128), BF16),
            pltpu.VMEM((1, 128), jnp.int32),
            pltpu.VMEM((1, 128), jnp.int32),
            pltpu.VMEM((2, 8, 2048), F32),
            pltpu.VMEM((8, 2048), F32),
            pltpu.VMEM((8, 2048), F32),
            pltpu.VMEM((1024, 128), F32),
            pltpu.VMEM((512, 128), BF16),
            pltpu.VMEM((3 * 512, 128), BF16),
        ]
        + [field] * 7
        + [
            pltpu.VMEM((5, 128, 128), F32),
            pltpu.VMEM((2, 5, 128, 128), F32),
            pltpu.VMEM((256, 128), BF16),
            pltpu.VMEM((256, 128), BF16),
            pltpu.VMEM((128, 128), BF16),
            pltpu.VMEM((256, 128), F32),
            dma((6,)),
            dma((15,)),
            dma((16,)),
            dma((8,)),
            dma((8,)),
            dma((2,)),
            dma((2,)),
            dma((8,)),
            dma((8,)),
            dma((15,)),
            dma((15,)),
            pltpu.SemaphoreType.REGULAR,
        ],
        compiler_params=pltpu.CompilerParams(
            collective_id=0, has_side_effects=True, vmem_limit_bytes=60 * 2**20
        ),
    )(
        ocean_forcing.reshape(512, 128),
        ice_owner,
        ice_mask,
        ice_velocity.reshape(2, 8, 2048),
        ice_mass.reshape(8, 2048),
        ice_strength.reshape(8, 2048),
    )
    return velocity.reshape(2, 1, 8, 2048), drag.reshape(1, 128, 2, 128)


def solution(mesh):
    in_specs = (
        P("face", "tile", None, None),
        P("face", "tile"),
        P("face", "tile"),
        P(None, "face", "tile", None),
        P("face", "tile", None),
        P("face", "tile", None),
    )
    out_specs = (P(None, "face", "tile", None), P("face", "tile", None, None))
    return jax.shard_map(
        per_device, mesh=mesh, in_specs=in_specs, out_specs=out_specs, check_vma=False
    )
```
